128 devices in a mesh: row: 8 (over y_lo, x), key: 16 (over z, y_hi, core).
Axes of the slice: x: 4, y: 4 (y_hi: 2, y_lo: 2; y = y_hi * 2 + y_lo), z: 4, core: 2. Of those that a mesh axis runs over, the one named last changes fastest.
Arguments:
- pair_window: bfloat16 [8, 4096, 128], P('row', 'key'), may hold values from -30 to 30
- ln_gain: float32 [128], replicated, may hold values from 0.1 to 1.9
- w_proj: bfloat16 [128, 512], replicated, may hold values from -0.5 to 0.5
- w_out: bfloat16 [128, 128], replicated, may hold values from -0.5 to 0.5
- pair_bias: bfloat16 [4, 4096, 4096], P(None, 'row', 'key'), may hold values from -10 to 330
- chain_starts: int32 [4], replicated, may hold values from 0 to 3072, as said below
- chain_pads: int32 [4], replicated, may hold values from 0 to 256, as said below
- residue_mask: int32 [4096], replicated, may hold values 0 or 1
Outputs:
- mixed: bfloat16 [8, 4096, 128], P('row', 'key')
The draws below stay inside these ranges and needn't reach their ends.
Inputs may be any that keep to these rules, and one draw needn't show every extreme that they name: `chain_starts`: strictly rising; the first is 0 and the last is 3072; the second and third lie 4096 // 8 to 1024 beyond the one before. `chain_pads`: some chain has exactly 256 padded positions.
All inputs are finite; a program needn't handle non-finite values.
Results may differ from the reference program's by a relative error of at most 0.0054.
The reference program's roundings to bfloat16 on the way count: a program that leaves them out, or rounds other values in their place, can miss the bound.
Values may be sent and summed in bfloat16 or wider, within the bound.
A program may use at most 192 MiB of HBM per device.

```python
import math
import jax
import jax.numpy as jnp
from jax import lax

C = 128
HEADS = 4
KEYBLK = 128
NCHAIN = 4
N = 4096
ROWS = 8
PAD_MOST = 256


def draw_pair_window(key, part):
    key = jax.random.fold_in(key, 7)
    target_shape = (ROWS, N, C)
    values = jax.random.normal(key, target_shape, jnp.float32)
    return jnp.clip(values, -30.0, 30.0).astype(jnp.bfloat16)


def draw_w_proj(key, part):
    key = jax.random.fold_in(key, 13)
    values = jax.random.normal(key, (C, 4 * C), jnp.float32) * C ** (-0.5)
    return jnp.clip(values, -0.5, 0.5).astype(jnp.bfloat16)


def draw_pair_bias(key, part):
    key = jax.random.fold_in(key, 11)
    target_shape = (HEADS, N, N)
    values = 2.5 * jax.random.normal(key, target_shape, jnp.float32)
    return jnp.clip(values, -10.0, 330.0).astype(jnp.bfloat16)


def draw_chain_starts(key, part):
    key = jax.random.fold_in(key, 3)
    spacing = jax.random.randint(key, (NCHAIN - 2,), N // 8, N // 4 + 1)
    middle = jnp.cumsum(spacing).astype(jnp.int32)
    return jnp.concatenate([jnp.zeros((1,), jnp.int32), middle, jnp.full((1,), 3 * (N // 4), jnp.int32)])


def draw_chain_pads(key, part):
    key = jax.random.fold_in(key, 5)
    streams = jax.random.split(key, 2)
    padding = jax.random.randint(streams[0], (NCHAIN,), 0, PAD_MOST + 1)
    widest = jax.random.randint(streams[1], (), 0, NCHAIN)
    return jnp.where(jnp.arange(NCHAIN) == widest, PAD_MOST, padding).astype(jnp.int32)


def touch_ends(values, stream_key, least, high):
    extent = values.shape
    place = [jax.random.randint(jax.random.fold_in(stream_key, axis), (), 0, extent[axis]) for axis in range(len(extent))]
    values = values.at[tuple(place)].set(least)
    longest = extent.index(max(extent))
    place[longest] = (place[longest] + 1) % extent[longest]
    return values.at[tuple(place)].set(high)


def noise(key, dims, width, reach, kind=jnp.bfloat16):
    array = jax.random.normal(key, dims, jnp.float32) * width
    return jnp.minimum(jnp.maximum(array, -reach), reach).astype(kind)


def setup_inputs(seed: int = 0) -> dict:
    keys = jax.random.split(jax.random.key(seed), 9)
    return {
        "pair_window": draw_pair_window(jax.random.fold_in(keys[8], 71), 0),
        "ln_gain": jnp.clip(1.0 + 0.18 * jax.random.normal(keys[1], (C,), jnp.float32), 0.1, 1.9),
        "w_proj": draw_w_proj(jax.random.fold_in(keys[8], 71), 0),
        "w_out": noise(keys[3], (C, C), C ** -0.5, 0.5),
        "pair_bias": draw_pair_bias(jax.random.fold_in(keys[8], 71), 0),
        "chain_starts": draw_chain_starts(jax.random.fold_in(keys[8], 71), 0),
        "chain_pads": draw_chain_pads(jax.random.fold_in(keys[8], 71), 0),
        "residue_mask": touch_ends((jax.random.randint(keys[7], (N,), 0, 16) < 15).astype(jnp.int32), jax.random.fold_in(keys[7], 1), 0, 1),
    }


epsilon = 1e-05
dead_score = -1000000000.0

def key_alive(chain_starts, chain_pads, residue_mask, length):
    places = jnp.arange(length, dtype=jnp.int32)
    chain_ends = jnp.concatenate([chain_starts[1:], jnp.full((1,), length, jnp.int32)]) - chain_pads
    inside = (places[:, None] >= chain_starts[None, :]) & (places[:, None] < chain_ends[None, :])
    leading = places[:, None] == chain_starts[None, :]
    return jnp.any(inside, axis=1) & ((residue_mask == 1) | jnp.any(leading, axis=1))

def project(pair_rows, ln_gain, w_proj):
    channels = pair_rows.shape[-1]
    head_width = channels // HEADS
    values = pair_rows.astype(jnp.float32)
    average = lax.optimization_barrier(jnp.mean(values, axis=-1, keepdims=True))
    centred = values - average
    variance = lax.optimization_barrier(jnp.mean(centred * centred, axis=-1, keepdims=True))
    normed = (centred * lax.rsqrt(variance + epsilon) * ln_gain.astype(jnp.float32)).astype(jnp.bfloat16)
    flat_rows = normed.reshape(-1, channels)
    projected = jnp.dot(flat_rows, w_proj, preferred_element_type=jnp.float32)
    factors = jnp.concatenate([jnp.full((channels,), head_width ** (-0.5), jnp.float32), jnp.ones((3 * channels,), jnp.float32)])
    return (projected * factors).astype(jnp.bfloat16).reshape(pair_rows.shape[:-1] + (4 * channels,))

def attend_row(query_rows, key_rows, value_rows, bias_tiles, alive_keys):
    length, channels = query_rows.shape
    head_width = channels // HEADS
    query_block = math.gcd(length, 512)
    blocks = length // KEYBLK
    query_tiles = query_rows.reshape(length // query_block, query_block, HEADS, head_width)
    key_table = key_rows.astype(jnp.float32).reshape(length, HEADS, head_width)
    value_table = value_rows.astype(jnp.float32).reshape(blocks, KEYBLK, HEADS, head_width)
    live_blocks = alive_keys.reshape(blocks, KEYBLK)

    def attend_tile(tile_pair):
        tile_queries, tile_bias = tile_pair
        scores = jnp.einsum('jhd,khd->hjk', tile_queries.astype(jnp.float32), key_table) + tile_bias.astype(jnp.float32)
        scores = scores.reshape(HEADS, query_block, blocks, KEYBLK)
        masked = jnp.where(live_blocks, scores, dead_score)
        block_max = lax.optimization_barrier(jnp.max(masked, axis=-1))
        weights = jnp.where(live_blocks, jnp.exp(masked - block_max[..., None]), 0.0)
        block_sum = lax.optimization_barrier(jnp.sum(weights, axis=-1))
        rounded = lax.optimization_barrier(weights.astype(jnp.bfloat16)).astype(jnp.float32)
        block_acc = jnp.einsum('hjbk,bkhd->hjbd', rounded, value_table)
        total_max = lax.optimization_barrier(jnp.max(block_max, axis=-1))
        factor = jnp.exp(block_max - total_max[..., None])
        total_sum = lax.optimization_barrier(jnp.sum(factor * block_sum, axis=-1))
        accum = lax.optimization_barrier(jnp.sum(factor[..., None] * block_acc, axis=2))
        attended = accum / total_sum[..., None]
        return jnp.transpose(attended, (1, 0, 2)).reshape(query_block, channels)
    return lax.map(attend_tile, (query_tiles, bias_tiles)).reshape(length, channels)

def reference(pair_window, ln_gain, w_proj, w_out, pair_bias, chain_starts, chain_pads, residue_mask):
    channels = pair_window.shape[-1]
    length = pair_window.shape[1]
    alive_keys = key_alive(chain_starts, chain_pads, residue_mask, length)
    query_block = math.gcd(length, 512)
    bias_tiles = jnp.transpose(pair_bias.reshape(HEADS, length // query_block, query_block, length), (1, 0, 2, 3))
    projected = project(pair_window, ln_gain, w_proj)

    def finish_row(packed):
        attended = attend_row(packed[:, :channels], packed[:, channels:2 * channels], packed[:, 2 * channels:3 * channels], bias_tiles, alive_keys)
        gate_rows = jax.nn.sigmoid(packed[:, 3 * channels:].astype(jnp.float32))
        gated_rows = (gate_rows * attended).astype(jnp.bfloat16)
        return jnp.dot(gated_rows, w_out, preferred_element_type=jnp.float32).astype(jnp.bfloat16)
    return lax.map(finish_row, projected)
```

```python
import functools

import jax
import jax.numpy as jnp
from jax import lax
from jax.experimental import pallas as pl
from jax.experimental.pallas import tpu as pltpu
from jax.sharding import PartitionSpec as P

HEADS = 4
KEYBLK = 128
WIDTH = 32
CH = 128
CHUNK = 256
NX, NYL, NZ, NYH = 4, 2, 4, 2
NR = NX * NYL
NM = NZ * NYH
STAT = HEADS * WIDTH
MSG = STAT + 2 * HEADS
MESH = pl.DeviceIdType.MESH
F32 = jnp.float32
BF16 = jnp.bfloat16

epsilon = 1e-05
dead_score = -1000000000.0
dead_bias = -1e30


def contract(a, b, dim_a, dim_b):
    return lax.dot_general(a, b, (((dim_a,), (dim_b,)), ((), ())), preferred_element_type=F32)


def shifts():
    return [(a, b) for b in range(NYL) for a in range(NX) if (a, b) != (0, 0)]


def kernel(
    starts_ref, pads_ref, x_ref, gain_ref, wqT_ref, wk_ref, wvT_ref, wgT_ref, w_out_ref, mask_ref, bias_ref, out_ref,
    nbuf, qbuf, braw, biasT, own, sbuf, rbuf,
    kv_ss, kv_rs, sib_ss, sib_rs, q_ss, q_rs, t_ss, bias_ss, bias_rs, bias_ls, home_ss, home_rs, home_ls,
):
    r = lax.axis_index("row")
    c = lax.axis_index("key")
    m = c // 2
    e = c % 2
    x, yl = r % NX, r // NX
    z, yh = m // NYH, m % NYH
    row_dev = lambda a, b: (((yl + b) % NYL) * NX + (x + a) % NX, c)
    key_dev = lambda a, b: (r, (((z + a) % NZ) * NYH + (yh + b) % NYH) * 2 + e)
    sib_dev = (r, m * 2 + 1 - e)
    diagonal = r == m

    def remote(src, dst, ss, rs, device):
        return pltpu.make_async_remote_copy(
            src_ref=src, dst_ref=dst, send_sem=ss, recv_sem=rs, device_id=device, device_id_type=MESH
        )

    barrier = pltpu.get_barrier_semaphore()
    pl.semaphore_signal(barrier, inc=1, device_id=sib_dev, device_id_type=MESH)
    for a, b in shifts():
        pl.semaphore_signal(barrier, inc=1, device_id=row_dev(a, b), device_id_type=MESH)
        pl.semaphore_signal(barrier, inc=1, device_id=key_dev(a, b), device_id_type=MESH)
    for k in range(NM):
        @pl.when(jnp.logical_not(diagonal & (m == k)))
        def _():
            pl.semaphore_signal(barrier, inc=1, device_id=(m, k * 2 + e), device_id_type=MESH)

    local_bias = pltpu.make_async_copy(bias_ref.at[:, pl.ds(pl.multiple_of(e * CHUNK, CHUNK), CHUNK), :], braw.at[e], bias_ls)
    local_bias.start()

    values = x_ref[0].astype(F32)
    average = jnp.mean(values, axis=-1, keepdims=True)
    centred = values - average
    variance = jnp.mean(centred * centred, axis=-1, keepdims=True)
    normed = (centred * lax.rsqrt(variance + epsilon) * gain_ref[...]).astype(BF16)
    own[...] = normed
    nbuf[r, e] = normed

    pl.semaphore_wait(barrier, 15 + jnp.where(diagonal, NR - 1, NR))

    q_send = remote(own, qbuf.at[r], t_ss, q_rs.at[r], (m, r * 2 + e))

    @pl.when(jnp.logical_not(diagonal))
    def _():
        q_send.start()

    @pl.when(diagonal)
    def _():
        qbuf[r] = own[...]

    kv_sends = [
        remote(own, nbuf.at[r, e], kv_ss.at[n], kv_rs.at[r], row_dev(a, b)) for n, (a, b) in enumerate(shifts())
    ]
    for send in kv_sends:
        send.start()
    remote(own, nbuf.at[r, e], sib_ss.at[r], sib_rs.at[r], sib_dev).start()
    bias_send = remote(
        bias_ref.at[:, pl.ds(pl.multiple_of((1 - e) * CHUNK, CHUNK), CHUNK), :], braw.at[e], bias_ss, bias_rs, sib_dev
    )
    bias_send.start()

    def forward(i):
        @pl.when(i != r)
        def _():
            remote(own, nbuf.at[i, e], kv_ss.at[0], kv_rs.at[i], sib_dev).wait_recv()
            remote(nbuf.at[i, e], nbuf.at[i, e], sib_ss.at[i], sib_rs.at[i], sib_dev).start()

    def turn_bias(core):
        for b in range(2):
            key0 = m * 512 + core * CHUNK + b * KEYBLK
            place = key0 + lax.broadcasted_iota(jnp.int32, (1, KEYBLK), 1)
            inside = jnp.zeros((1, KEYBLK), jnp.bool_)
            leading = jnp.zeros((1, KEYBLK), jnp.bool_)
            for n in range(4):
                start = starts_ref[n]
                end = (starts_ref[n + 1] if n < 3 else 4096) - pads_ref[n]
                inside = inside | ((place >= start) & (place < end))
                leading = leading | (place == start)
            alive = inside & ((mask_ref[m, pl.ds(core * 2 + b, 1), :] == 1) | leading)
            for h in range(HEADS):
                piece = braw[core, h, :, b * KEYBLK : (b + 1) * KEYBLK].astype(F32)
                piece = jnp.where(alive, piece, dead_bias)
                biasT[h, pl.ds(pl.multiple_of(core * CHUNK + b * KEYBLK, KEYBLK), KEYBLK), :] = piece.T

    local_bias.wait()
    turn_bias(e)

    @pl.when(jnp.logical_not(diagonal))
    def _():
        remote(own, qbuf.at[m], t_ss, q_rs.at[m], sib_dev).wait_recv()

    q_sends = [
        remote(qbuf.at[m], qbuf.at[m], q_ss.at[n], q_rs.at[m], key_dev(a, b)) for n, (a, b) in enumerate(shifts())
    ]
    for send in q_sends:
        send.start()
    bias_send.wait_recv()
    turn_bias(1 - e)
    forward(m)

    def step(s, carry):
        i = (m + s) % NR

        @pl.when(s < NR - 1)
        def _():
            forward((i + 1) % NR)

        remote(own, nbuf.at[i, 1 - e], kv_ss.at[0], sib_rs.at[i], sib_dev).wait_recv()

        @pl.when(s > 0)
        def _():
            remote(own, qbuf.at[i], kv_ss.at[0], q_rs.at[i], sib_dev).wait_recv()

        rows = nbuf[i].reshape(2 * CHUNK, CH)
        keys = jnp.dot(rows, wk_ref[...], preferred_element_type=F32).astype(BF16)
        valuesT = contract(wvT_ref[...], rows, 1, 1).astype(BF16)
        queriesT = (contract(wqT_ref[...], qbuf[i], 1, 1) * (WIDTH**-0.5)).astype(BF16)
        for h in range(HEADS):
            low = h * WIDTH
            parts = []
            if low:
                parts.append(jnp.zeros((low, CHUNK), BF16))
            parts.append(queriesT[low : low + WIDTH])
            if low + WIDTH < CH:
                parts.append(jnp.zeros((CH - low - WIDTH, CHUNK), BF16))
            one_head = jnp.concatenate(parts, axis=0)
            maxima, sums, accs = [], [], []
            for b in range(4):
                k0 = b * KEYBLK
                scores = jnp.dot(keys[k0 : k0 + KEYBLK], one_head, preferred_element_type=F32)
                scores = scores + biasT[h, k0 : k0 + KEYBLK, :]
                block_max = jnp.maximum(jnp.max(scores, axis=0, keepdims=True), dead_score)
                weights = jnp.exp(scores - block_max)
                sums.append(jnp.sum(weights, axis=0, keepdims=True))
                accs.append(
                    jnp.dot(valuesT[low : low + WIDTH, k0 : k0 + KEYBLK], weights.astype(BF16), preferred_element_type=F32)
                )
                maxima.append(block_max)
            top = functools.reduce(jnp.maximum, maxima)
            factors = [jnp.exp(v - top) for v in maxima]
            total = sum(f * v for f, v in zip(factors, sums))
            accum = sum(f * v for f, v in zip(factors, accs))
            sbuf[i, low : low + WIDTH, :] = accum
            sbuf[i, STAT + h : STAT + h + 1, :] = top
            sbuf[i, STAT + HEADS + h : STAT + HEADS + h + 1, :] = total

        at_home = diagonal & (i == r)

        @pl.when(at_home)
        def _():
            pltpu.make_async_copy(sbuf.at[i], rbuf.at[m], home_ls).start()

        @pl.when(jnp.logical_not(at_home))
        def _():
            remote(sbuf.at[i], rbuf.at[m], home_ss.at[i], home_rs.at[m], (i, r * 2 + e)).start()

        return carry

    lax.fori_loop(0, NR, step, 0)

    gatesT = contract(wgT_ref[...], own[...], 1, 1).astype(BF16).astype(F32)

    for k in range(NM):
        is_self = diagonal & (m == k)

        @pl.when(is_self)
        def _():
            pltpu.make_async_copy(sbuf.at[k], rbuf.at[k], home_ls).wait()

        @pl.when(jnp.logical_not(is_self))
        def _():
            remote(sbuf.at[k], rbuf.at[k], home_ss.at[k], home_rs.at[k], sib_dev).wait_recv()

    gated = []
    for h in range(HEADS):
        low = h * WIDTH
        tops = [rbuf[k, STAT + h : STAT + h + 1, :] for k in range(NM)]
        top = functools.reduce(jnp.maximum, tops)
        factors = [jnp.exp(v - top) for v in tops]
        total = sum(f * rbuf[k, STAT + HEADS + h : STAT + HEADS + h + 1, :] for k, f in enumerate(factors))
        accum = sum(f * rbuf[k, low : low + WIDTH, :] for k, f in enumerate(factors))
        attended = accum / total
        gate = 1.0 / (1.0 + jnp.exp(-gatesT[low : low + WIDTH]))
        gated.append((gate * attended).astype(BF16))
    gatedT = jnp.concatenate(gated, axis=0)
    out_ref[0] = contract(gatedT, w_out_ref[...], 0, 0).astype(BF16)

    for send in kv_sends + q_sends:
        send.wait_send()
    bias_send.wait_send()

    @pl.when(jnp.logical_not(diagonal))
    def _():
        q_send.wait_send()

    for k in range(NR):
        remote(own, nbuf.at[k, e], sib_ss.at[k], sib_rs.at[k], sib_dev).wait_send()

        @pl.when(jnp.logical_not(diagonal & (m == k)))
        def _():
            remote(sbuf.at[k], rbuf.at[k], home_ss.at[k], home_rs.at[k], sib_dev).wait_send()


def local(pair_window, ln_gain, w_proj, w_out, pair_bias, chain_starts, chain_pads, residue_mask):
    vmem = pl.BlockSpec(memory_space=pltpu.VMEM)
    smem = pl.BlockSpec(memory_space=pltpu.SMEM)
    dma = pltpu.SemaphoreType.DMA
    wT = w_proj.T
    return pl.pallas_call(
        kernel,
        out_shape=jax.ShapeDtypeStruct((1, CHUNK, CH), BF16),
        in_specs=[smem, smem] + [vmem] * 8 + [pl.BlockSpec(memory_space=pl.ANY)],
        out_specs=vmem,
        scratch_shapes=[
            pltpu.VMEM((NR, 2, CHUNK, CH), BF16),
            pltpu.VMEM((NR, CHUNK, CH), BF16),
            pltpu.VMEM((2, HEADS, CHUNK, CHUNK), BF16),
            pltpu.VMEM((HEADS, 2 * CHUNK, CHUNK), F32),
            pltpu.VMEM((CHUNK, CH), BF16),
            pltpu.VMEM((NR, MSG, CHUNK), F32),
            pltpu.VMEM((NM, MSG, CHUNK), F32),
            dma((7,)), dma((NR,)), dma((NR,)), dma((NR,)), dma((7,)), dma((NR,)), dma, dma, dma, dma,
            dma((NR,)), dma((NM,)), dma,
        ],
        compiler_params=pltpu.CompilerParams(
            collective_id=0, has_side_effects=True, vmem_limit_bytes=40 * 2**20
        ),
        name="triangle",
    )(
        chain_starts, chain_pads, pair_window, ln_gain.reshape(1, CH), wT[:CH], w_proj[:, CH : 2 * CH],
        wT[2 * CH : 3 * CH], wT[3 * CH :], w_out, residue_mask.reshape(NM, 4, 128), pair_bias,
    )


def solution(mesh):
    in_specs = (P("row", "key", None), P(), P(), P(), P(None, "row", "key"), P(), P(), P())
    out_specs = P("row", "key", None)
    return jax.shard_map(local, mesh=mesh, in_specs=in_specs, out_specs=out_specs, check_vma=False)
```

```python
import functools

import jax
import jax.numpy as jnp
from jax import lax
from jax.experimental import pallas as pl
from jax.experimental.pallas import tpu as pltpu
from jax.sharding import PartitionSpec as P

HEADS = 4
KEYBLK = 128
WIDTH = 32
CH = 128
CHUNK = 256
KEYS = 2 * CHUNK
NBLK = KEYS // KEYBLK
NX, NYL, NZ, NYH = 4, 2, 4, 2
NR = NX * NYL
NM = NZ * NYH
NCHAIN = 4
LENGTH = 4096
STATS = 16
STEPS = 32767.0
MESH = pl.DeviceIdType.MESH
F32 = jnp.float32
BF16 = jnp.bfloat16

epsilon = 1e-05
dead_score = -1000000000.0
dead_bias = -1e30


def contract(a, b, dim_a, dim_b):
    return lax.dot_general(a, b, (((dim_a,), (dim_b,)), ((), ())), preferred_element_type=F32)


def kernel(
    starts_ref, pads_ref, x_hbm, gain_hbm, w_hbm, w_out_hbm, mask_hbm, bias_ref, out_ref,
    x_ref, gain_ref, w_ref, w_out_ref, mask_ref,
    nbuf, qbuf, braw, biasT, own, wqT, wvT, wgT, s_scr, p_scr, sbuf, sstat, rbuf, rstat,
    in_sem, kv_ss, kv_rs, sib_ss, sib_rs, q_ss, q_rs, t_ss, bias_ss, bias_rs, bias_ls, home_ss, home_rs, home_ls,
    stat_ss, stat_rs, stat_ls,
):
    r = lax.axis_index("row")
    c = lax.axis_index("key")
    m = c // 2
    e = c % 2
    x, yl = r % NX, r // NX
    z, yh = m // NYH, m % NYH
    row_at = lambda a, b: ((yl + b) % NYL) * NX + (x + a) % NX
    key_at = lambda a, b: ((z + a) % NZ) * NYH + (yh + b) % NYH
    row_dev = lambda a, b: (row_at(a, b), c)
    key_dev = lambda a, b: (r, key_at(a, b) * 2 + e)
    sib_dev = (r, m * 2 + 1 - e)
    diagonal = r == m

    def remote(src, dst, ss, rs, device):
        return pltpu.make_async_remote_copy(
            src_ref=src, dst_ref=dst, send_sem=ss, recv_sem=rs, device_id=device, device_id_type=MESH
        )

    loads = [
        pltpu.make_async_copy(src, dst, in_sem.at[n])
        for n, (src, dst) in enumerate(
            ((x_hbm, x_ref), (gain_hbm, gain_ref), (w_hbm, w_ref), (w_out_hbm, w_out_ref), (mask_hbm, mask_ref))
        )
    ]
    for load in loads:
        load.start()
    local_bias = pltpu.make_async_copy(bias_ref.at[:, pl.ds(pl.multiple_of(e * CHUNK, CHUNK), CHUNK), :], braw.at[e], bias_ls)
    local_bias.start()

    barrier = pltpu.get_barrier_semaphore()
    pl.semaphore_signal(barrier, inc=1, device_id=sib_dev, device_id_type=MESH)
    for a, b in ((1, 0), (2, 0), (3, 0), (0, 1)):
        pl.semaphore_signal(barrier, inc=1, device_id=row_dev(a, b), device_id_type=MESH)
        pl.semaphore_signal(barrier, inc=1, device_id=key_dev(a, b), device_id_type=MESH)
    for k in range(NM):
        @pl.when(jnp.logical_not(diagonal & (m == k)))
        def _():
            pl.semaphore_signal(barrier, inc=1, device_id=(m, k * 2 + e), device_id_type=MESH)

    loads[0].wait()
    loads[1].wait()
    values = x_ref[0].astype(F32)
    average = jnp.mean(values, axis=-1, keepdims=True)
    centred = values - average
    variance = jnp.mean(centred * centred, axis=-1, keepdims=True)
    normed = (centred * lax.rsqrt(variance + epsilon) * gain_ref[...]).astype(BF16)
    own[...] = normed
    nbuf[r, e] = normed

    pl.semaphore_wait(barrier, 9 + jnp.where(diagonal, NR - 1, NR))

    q_send = remote(own, qbuf.at[r], t_ss, q_rs.at[r], (m, r * 2 + e))

    @pl.when(jnp.logical_not(diagonal))
    def _():
        q_send.start()

    @pl.when(diagonal)
    def _():
        qbuf[r] = own[...]

    partner = row_at(0, 1)
    kv_sends = [remote(own, nbuf.at[r, e], kv_ss.at[0], kv_rs.at[r], row_dev(0, 1))]
    kv_sends += [remote(own, nbuf.at[r, e], kv_ss.at[a], kv_rs.at[r], row_dev(a, 0)) for a in (1, 3, 2)]
    for send in kv_sends:
        send.start()
    remote(own, nbuf.at[r, e], sib_ss.at[r], sib_rs.at[r], sib_dev).start()
    bias_send = remote(
        bias_ref.at[:, pl.ds(pl.multiple_of((1 - e) * CHUNK, CHUNK), CHUNK), :], braw.at[e], bias_ss, bias_rs, sib_dev
    )
    bias_send.start()

    def arrived(i):
        remote(own, nbuf.at[i, e], kv_ss.at[0], kv_rs.at[i], sib_dev).wait_recv()

    def to_sibling(i):
        @pl.when((i != r) & (i != partner))
        def _():
            arrived(i)
            remote(nbuf.at[i, e], nbuf.at[i, e], sib_ss.at[i], sib_rs.at[i], sib_dev).start()

    loads[2].wait()
    for ref, low in ((wqT, 0), (wvT, 2 * CH), (wgT, 3 * CH)):
        ref[...] = w_ref[:, low : low + CH].astype(F32).T.astype(BF16)
    loads[4].wait()

    def turn_bias(core):
        for b in range(2):
            key0 = m * KEYS + core * CHUNK + b * KEYBLK
            place = key0 + lax.broadcasted_iota(jnp.int32, (1, KEYBLK), 1)
            inside = jnp.zeros((1, KEYBLK), jnp.bool_)
            leading = jnp.zeros((1, KEYBLK), jnp.bool_)
            for n in range(NCHAIN):
                start = starts_ref[n]
                end = (starts_ref[n + 1] if n < NCHAIN - 1 else LENGTH) - pads_ref[n]
                inside = inside | ((place >= start) & (place < end))
                leading = leading | (place == start)
            alive = inside & ((mask_ref[pl.ds(m * NBLK + core * 2 + b, 1), :] == 1) | leading)
            for h in range(HEADS):
                piece = braw[core, h, :, b * KEYBLK : (b + 1) * KEYBLK].astype(F32)
                piece = jnp.where(alive, piece, dead_bias)
                biasT[h, pl.ds(pl.multiple_of(core * CHUNK + b * KEYBLK, KEYBLK), KEYBLK), :] = piece.T

    local_bias.wait()
    turn_bias(e)

    arrived(partner)
    kv_ons = [remote(nbuf.at[partner, e], nbuf.at[partner, e], kv_ss.at[3 + a], kv_rs.at[partner], row_dev(a, 0)) for a in (1, 3, 2)]
    for send in kv_ons:
        send.start()
    remote(nbuf.at[partner, e], nbuf.at[partner, e], sib_ss.at[partner], sib_rs.at[partner], sib_dev).start()

    def q_arrived(i):
        remote(own, qbuf.at[i], t_ss, q_rs.at[i], sib_dev).wait_recv()

    @pl.when(jnp.logical_not(diagonal))
    def _():
        q_arrived(m)

    q_sends = [remote(qbuf.at[m], qbuf.at[m], q_ss.at[0], q_rs.at[m], key_dev(0, 1))]
    q_sends += [remote(qbuf.at[m], qbuf.at[m], q_ss.at[a], q_rs.at[m], key_dev(a, 0)) for a in (1, 3, 2)]
    for send in q_sends:
        send.start()
    bias_send.wait_recv()
    turn_bias(1 - e)
    to_sibling(m)

    other = key_at(0, 1)
    q_arrived(other)
    q_ons = [remote(qbuf.at[other], qbuf.at[other], q_ss.at[3 + a], q_rs.at[other], key_dev(a, 0)) for a in (1, 3, 2)]
    for send in q_ons:
        send.start()

    def turn(s):
        return ((z + s) % NZ) * NYH + (yh + s // NZ) % NYH

    def step(s, carry):
        i = turn(s)

        @pl.when(s < NR - 1)
        def _():
            to_sibling(turn(s + 1))

        remote(own, nbuf.at[i, 1 - e], kv_ss.at[0], sib_rs.at[i], sib_dev).wait_recv()

        @pl.when((s > 0) & (s != NZ))
        def _():
            q_arrived(i)

        rows = nbuf[i].reshape(KEYS, CH)
        keys = jnp.dot(rows, w_ref[:, CH : 2 * CH], preferred_element_type=F32).astype(BF16)
        valuesT = contract(wvT[...], rows, 1, 1).astype(BF16)
        queriesT = (contract(wqT[...], qbuf[i], 1, 1) * (WIDTH**-0.5)).astype(BF16)
        tops, sums = {}, {}

        def phase_scores(h):
            low = h * WIDTH
            parts = []
            if low:
                parts.append(jnp.zeros((low, CHUNK), BF16))
            parts.append(queriesT[low : low + WIDTH])
            if low + WIDTH < CH:
                parts.append(jnp.zeros((CH - low - WIDTH, CHUNK), BF16))
            one_head = jnp.concatenate(parts, axis=0)
            scores = jnp.dot(keys, one_head, preferred_element_type=F32)
            tops[h] = []
            for b in range(NBLK):
                k0 = b * KEYBLK
                part = scores[k0 : k0 + KEYBLK] + biasT[h, k0 : k0 + KEYBLK, :]
                s_scr[h, k0 : k0 + KEYBLK, :] = part
                tops[h].append(jnp.maximum(jnp.max(part, axis=0, keepdims=True), dead_score))

        def phase_weights(h):
            sums[h] = []
            for b in range(NBLK):
                k0 = b * KEYBLK
                weights = jnp.exp(s_scr[h, k0 : k0 + KEYBLK, :] - tops[h][b])
                sums[h].append(jnp.sum(weights, axis=0, keepdims=True))
                p_scr[h, k0 : k0 + KEYBLK, :] = weights.astype(BF16)

        def phase_values(h):
            low = h * WIDTH
            accs = []
            for b in range(NBLK):
                k0 = b * KEYBLK
                accs.append(
                    jnp.dot(valuesT[low : low + WIDTH, k0 : k0 + KEYBLK], p_scr[h, k0 : k0 + KEYBLK, :], preferred_element_type=F32)
                )
            top = functools.reduce(jnp.maximum, tops[h])
            factors = [jnp.exp(v - top) for v in tops[h]]
            total = sum(f * v for f, v in zip(factors, sums[h]))
            accum = sum(f * v for f, v in zip(factors, accs))
            reach = jnp.maximum(jnp.max(jnp.abs(accum), axis=0, keepdims=True), 1e-30)
            sbuf[i, low : low + WIDTH, :] = jnp.round(accum * (STEPS / reach)).astype(jnp.int32).astype(jnp.int16)
            sstat[i, h : h + 1, :] = top
            sstat[i, HEADS + h : HEADS + h + 1, :] = total
            sstat[i, 2 * HEADS + h : 2 * HEADS + h + 1, :] = reach * (1.0 / STEPS)

        for t in range(HEADS + 2):
            if t < HEADS:
                phase_scores(t)
            if 0 <= t - 1 < HEADS:
                phase_weights(t - 1)
            if 0 <= t - 2 < HEADS:
                phase_values(t - 2)

        at_home = diagonal & (i == r)

        @pl.when(at_home)
        def _():
            pltpu.make_async_copy(sbuf.at[i], rbuf.at[m], home_ls).start()
            pltpu.make_async_copy(sstat.at[i], rstat.at[m], stat_ls).start()

        @pl.when(jnp.logical_not(at_home))
        def _():
            remote(sbuf.at[i], rbuf.at[m], home_ss.at[i], home_rs.at[m], (i, r * 2 + e)).start()
            remote(sstat.at[i], rstat.at[m], stat_ss.at[i], stat_rs.at[m], (i, r * 2 + e)).start()

        return carry

    sstat[:, 3 * HEADS :, :] = jnp.zeros((NR, STATS - 3 * HEADS, CHUNK), F32)
    lax.fori_loop(0, NR, step, 0)

    gatesT = contract(wgT[...], own[...], 1, 1).astype(BF16).astype(F32)
    gates = 1.0 / (1.0 + jnp.exp(-gatesT))
    loads[3].wait()

    for k in range(NM):
        is_self = diagonal & (m == k)

        @pl.when(is_self)
        def _():
            pltpu.make_async_copy(sbuf.at[k], rbuf.at[k], home_ls).wait()
            pltpu.make_async_copy(sstat.at[k], rstat.at[k], stat_ls).wait()

        @pl.when(jnp.logical_not(is_self))
        def _():
            remote(sbuf.at[k], rbuf.at[k], home_ss.at[k], home_rs.at[k], sib_dev).wait_recv()
            remote(sstat.at[k], rstat.at[k], stat_ss.at[k], stat_rs.at[k], sib_dev).wait_recv()

    gated = []
    for h in range(HEADS):
        low = h * WIDTH
        tops = [rstat[k, h : h + 1, :] for k in range(NM)]
        top = functools.reduce(jnp.maximum, tops)
        factors = [jnp.exp(v - top) for v in tops]
        total = sum(f * rstat[k, HEADS + h : HEADS + h + 1, :] for k, f in enumerate(factors))
        accum = sum(
            (f * rstat[k, 2 * HEADS + h : 2 * HEADS + h + 1, :]) * rbuf[k, low : low + WIDTH, :].astype(jnp.int32).astype(F32)
            for k, f in enumerate(factors)
        )
        gated.append((gates[low : low + WIDTH] * (accum / total)).astype(BF16))
    gatedT = jnp.concatenate(gated, axis=0)
    out_ref[0] = contract(gatedT, w_out_ref[...], 0, 0).astype(BF16)

    for send in kv_sends + kv_ons + q_sends + q_ons:
        send.wait_send()
    bias_send.wait_send()

    @pl.when(jnp.logical_not(diagonal))
    def _():
        q_send.wait_send()

    for k in range(NR):
        remote(own, nbuf.at[k, e], sib_ss.at[k], sib_rs.at[k], sib_dev).wait_send()

        @pl.when(jnp.logical_not(diagonal & (m == k)))
        def _():
            remote(sbuf.at[k], rbuf.at[k], home_ss.at[k], home_rs.at[k], sib_dev).wait_send()
            remote(sstat.at[k], rstat.at[k], stat_ss.at[k], stat_rs.at[k], sib_dev).wait_send()


def local(pair_window, ln_gain, w_proj, w_out, pair_bias, chain_starts, chain_pads, residue_mask):
    vmem = pl.BlockSpec(memory_space=pltpu.VMEM)
    smem = pl.BlockSpec(memory_space=pltpu.SMEM)
    hbm = pl.BlockSpec(memory_space=pl.ANY)
    dma = pltpu.SemaphoreType.DMA
    return pl.pallas_call(
        kernel,
        out_shape=jax.ShapeDtypeStruct((1, CHUNK, CH), BF16),
        in_specs=[smem, smem] + [hbm] * 6,
        out_specs=vmem,
        scratch_shapes=[
            pltpu.VMEM((1, CHUNK, CH), BF16),
            pltpu.VMEM((1, CH), F32),
            pltpu.VMEM((CH, 4 * CH), BF16),
            pltpu.VMEM((CH, CH), BF16),
            pltpu.VMEM((LENGTH // KEYBLK, KEYBLK), jnp.int32),
            pltpu.VMEM((NR, 2, CHUNK, CH), BF16),
            pltpu.VMEM((NR, CHUNK, CH), BF16),
            pltpu.VMEM((2, HEADS, CHUNK, CHUNK), BF16),
            pltpu.VMEM((HEADS, KEYS, CHUNK), F32),
            pltpu.VMEM((CHUNK, CH), BF16),
            pltpu.VMEM((CH, CH), BF16),
            pltpu.VMEM((CH, CH), BF16),
            pltpu.VMEM((CH, CH), BF16),
            pltpu.VMEM((HEADS, KEYS, CHUNK), F32),
            pltpu.VMEM((HEADS, KEYS, CHUNK), BF16),
            pltpu.VMEM((NR, CH, CHUNK), jnp.int16),
            pltpu.VMEM((NR, STATS, CHUNK), F32),
            pltpu.VMEM((NM, CH, CHUNK), jnp.int16),
            pltpu.VMEM((NM, STATS, CHUNK), F32),
            dma((5,)), dma((7,)), dma((NR,)), dma((NR,)), dma((NR,)), dma((7,)), dma((NR,)), dma, dma, dma, dma,
            dma((NR,)), dma((NM,)), dma, dma((NR,)), dma((NM,)), dma,
        ],
        compiler_params=pltpu.CompilerParams(
            collective_id=0, has_side_effects=True, vmem_limit_bytes=60 * 2**20
        ),
        name="triangle",
    )(
        chain_starts, chain_pads, pair_window, ln_gain.reshape(1, CH), w_proj, w_out,
        residue_mask.reshape(LENGTH // KEYBLK, KEYBLK), pair_bias,
    )


def solution(mesh):
    in_specs = (P("row", "key", None), P(), P(), P(), P(None, "row", "key"), P(), P(), P())
    out_specs = P("row", "key", None)
    return jax.shard_map(local, mesh=mesh, in_specs=in_specs, out_specs=out_specs, check_vma=False)
```

```python
import functools

import jax
import jax.numpy as jnp
from jax import lax
from jax.experimental import pallas as pl
from jax.experimental.pallas import tpu as pltpu
from jax.sharding import PartitionSpec as P

HEADS = 4
KEYBLK = 128
WIDTH = 32
CH = 128
CHUNK = 256
KEYS = 2 * CHUNK
NBLK = KEYS // KEYBLK
NX, NYL, NZ, NYH = 4, 2, 4, 2
NR = NX * NYL
NM = NZ * NYH
NCHAIN = 4
LENGTH = 4096
STATS = 16
STEPS = 32767.0
MESH = pl.DeviceIdType.MESH
F32 = jnp.float32
BF16 = jnp.bfloat16

epsilon = 1e-05
dead_score = -1000000000.0
dead_bias = -1e30


def contract(a, b, dim_a, dim_b):
    return lax.dot_general(a, b, (((dim_a,), (dim_b,)), ((), ())), preferred_element_type=F32)


def kernel(
    starts_ref, pads_ref, x_hbm, gain_hbm, w_hbm, w_out_hbm, mask_hbm, bias_ref, out_ref,
    x_ref, gain_ref, w_ref, w_out_ref, mask_ref,
    nbuf, qbuf, braw, biasT, own, wqT, wvT, wgT, s_scr, p_scr, sbuf, sstat, rbuf, rstat, merged,
    in_sem, kv_ss, kv_rs, sib_ss, sib_rs, q_ss, q_rs, t_ss, bias_ss, bias_rs, bias_ls, home_ss, home_rs, home_ls,
    stat_ss, stat_rs, stat_ls,
):
    r = lax.axis_index("row")
    c = lax.axis_index("key")
    m = c // 2
    e = c % 2
    x, yl = r % NX, r // NX
    z, yh = m // NYH, m % NYH
    row_at = lambda a, b: ((yl + b) % NYL) * NX + (x + a) % NX
    key_at = lambda a, b: ((z + a) % NZ) * NYH + (yh + b) % NYH
    row_dev = lambda a, b: (row_at(a, b), c)
    key_dev = lambda a, b: (r, key_at(a, b) * 2 + e)
    sib_dev = (r, m * 2 + 1 - e)
    diagonal = r == m

    def remote(src, dst, ss, rs, device):
        return pltpu.make_async_remote_copy(
            src_ref=src, dst_ref=dst, send_sem=ss, recv_sem=rs, device_id=device, device_id_type=MESH
        )

    loads = [
        pltpu.make_async_copy(src, dst, in_sem.at[n])
        for n, (src, dst) in enumerate(
            ((x_hbm, x_ref), (gain_hbm, gain_ref), (w_hbm, w_ref), (w_out_hbm, w_out_ref), (mask_hbm, mask_ref))
        )
    ]
    loads[0].start()
    loads[1].start()
    local_bias = pltpu.make_async_copy(bias_ref.at[:, pl.ds(pl.multiple_of(e * CHUNK, CHUNK), CHUNK), :], braw.at[e], bias_ls)

    barrier = pltpu.get_barrier_semaphore()
    pl.semaphore_signal(barrier, inc=1, device_id=sib_dev, device_id_type=MESH)
    for a, b in ((1, 0), (2, 0), (3, 0), (0, 1)):
        pl.semaphore_signal(barrier, inc=1, device_id=row_dev(a, b), device_id_type=MESH)
        pl.semaphore_signal(barrier, inc=1, device_id=key_dev(a, b), device_id_type=MESH)
    for k in range(NM):
        @pl.when(jnp.logical_not(diagonal & (m == k)))
        def _():
            pl.semaphore_signal(barrier, inc=1, device_id=(m, k * 2 + e), device_id_type=MESH)

    for load in loads[2:] + [local_bias]:
        load.start()

    loads[0].wait()
    loads[1].wait()
    values = x_ref[0].astype(F32)
    average = jnp.mean(values, axis=-1, keepdims=True)
    centred = values - average
    variance = jnp.mean(centred * centred, axis=-1, keepdims=True)
    normed = (centred * lax.rsqrt(variance + epsilon) * gain_ref[...]).astype(BF16)
    own[...] = normed
    nbuf[r, e] = normed

    pl.semaphore_wait(barrier, 9 + jnp.where(diagonal, NR - 1, NR))

    HALF = CHUNK // 2
    halves = [pl.ds(n * HALF, HALF) for n in range(2)]
    t_sends = [remote(own.at[v], qbuf.at[r, v], t_ss.at[n], q_rs.at[n, r], (m, r * 2 + e)) for n, v in enumerate(halves)]

    @pl.when(jnp.logical_not(diagonal))
    def _():
        for send in t_sends:
            send.start()

    @pl.when(diagonal)
    def _():
        qbuf[r] = own[...]

    partner = row_at(0, 1)
    kv_sends = [remote(own, nbuf.at[r, e], kv_ss.at[0], kv_rs.at[r], row_dev(0, 1))]
    kv_sends += [remote(own, nbuf.at[r, e], kv_ss.at[a], kv_rs.at[r], row_dev(a, 0)) for a in (1, 3, 2)]
    for send in kv_sends:
        send.start()
    remote(own, nbuf.at[r, e], sib_ss.at[r], sib_rs.at[r], sib_dev).start()
    bias_send = remote(
        bias_ref.at[:, pl.ds(pl.multiple_of((1 - e) * CHUNK, CHUNK), CHUNK), :], braw.at[e], bias_ss, bias_rs, sib_dev
    )
    bias_send.start()

    def arrived(i):
        remote(own, nbuf.at[i, e], kv_ss.at[0], kv_rs.at[i], sib_dev).wait_recv()

    def to_sibling(i):
        arrived(i)
        remote(nbuf.at[i, e], nbuf.at[i, e], sib_ss.at[i], sib_rs.at[i], sib_dev).start()

    loads[2].wait()
    for ref, low in ((wqT, 0), (wvT, 2 * CH), (wgT, 3 * CH)):
        ref[...] = w_ref[:, low : low + CH].astype(F32).T.astype(BF16)
    loads[4].wait()

    def turn_bias(core):
        for b in range(2):
            key0 = m * KEYS + core * CHUNK + b * KEYBLK
            place = key0 + lax.broadcasted_iota(jnp.int32, (1, KEYBLK), 1)
            inside = jnp.zeros((1, KEYBLK), jnp.bool_)
            leading = jnp.zeros((1, KEYBLK), jnp.bool_)
            for n in range(NCHAIN):
                start = starts_ref[n]
                end = (starts_ref[n + 1] if n < NCHAIN - 1 else LENGTH) - pads_ref[n]
                inside = inside | ((place >= start) & (place < end))
                leading = leading | (place == start)
            alive = inside & ((mask_ref[pl.ds(m * NBLK + core * 2 + b, 1), :] == 1) | leading)
            for h in range(HEADS):
                piece = braw[core, h, :, b * KEYBLK : (b + 1) * KEYBLK].astype(F32)
                piece = jnp.where(alive, piece, dead_bias)
                biasT[h, pl.ds(pl.multiple_of(core * CHUNK + b * KEYBLK, KEYBLK), KEYBLK), :] = piece.T

    local_bias.wait()
    turn_bias(e)

    arrived(partner)
    kv_ons = [remote(nbuf.at[partner, e], nbuf.at[partner, e], kv_ss.at[3 + a], kv_rs.at[partner], row_dev(a, 0)) for a in (1, 3, 2)]
    for send in kv_ons:
        send.start()
    remote(nbuf.at[partner, e], nbuf.at[partner, e], sib_ss.at[partner], sib_rs.at[partner], sib_dev).start()

    def q_arrived(i, n):
        remote(own.at[halves[n]], qbuf.at[i, halves[n]], t_ss.at[0], q_rs.at[n, i], sib_dev).wait_recv()

    def q_copy(i, n, slot, device):
        v = qbuf.at[i, halves[n]]
        return remote(v, v, q_ss.at[n, slot], q_rs.at[n, i], device)

    q_sends = []
    for n in range(2):
        @pl.when(jnp.logical_not(diagonal))
        def _():
            q_arrived(m, n)

        now = [q_copy(m, n, 0, key_dev(0, 1))] + [q_copy(m, n, a, key_dev(a, 0)) for a in (1, 3, 2)]
        for send in now:
            send.start()
        q_sends += now
    bias_send.wait_recv()
    turn_bias(1 - e)
    for a, b in ((1, 0), (3, 0), (2, 0), (1, 1), (3, 1), (2, 1)):
        to_sibling(row_at(a, b))

    other = key_at(0, 1)
    q_ons = []
    for n in range(2):
        q_arrived(other, n)
        now = [q_copy(other, n, 3 + a, key_dev(a, 0)) for a in (1, 3, 2)]
        for send in now:
            send.start()
        q_ons += now

    def turn(s):
        return ((z + s) % NZ) * NYH + (yh + s // NZ) % NYH

    def step(s, carry):
        i = turn(s)

        remote(own, nbuf.at[i, 1 - e], kv_ss.at[0], sib_rs.at[i], sib_dev).wait_recv()

        @pl.when((s > 0) & (s != NZ))
        def _():
            q_arrived(i, 0)
            q_arrived(i, 1)

        rows = nbuf[i].reshape(KEYS, CH)
        keys = jnp.dot(rows, w_ref[:, CH : 2 * CH], preferred_element_type=F32).astype(BF16)
        valuesT = contract(wvT[...], rows, 1, 1).astype(BF16)
        queriesT = (contract(wqT[...], qbuf[i], 1, 1) * (WIDTH**-0.5)).astype(BF16)
        tops, sums = {}, {}

        def phase_scores(h):
            low = h * WIDTH
            parts = []
            if low:
                parts.append(jnp.zeros((low, CHUNK), BF16))
            parts.append(queriesT[low : low + WIDTH])
            if low + WIDTH < CH:
                parts.append(jnp.zeros((CH - low - WIDTH, CHUNK), BF16))
            one_head = jnp.concatenate(parts, axis=0)
            scores = jnp.dot(keys, one_head, preferred_element_type=F32)
            tops[h] = []
            for b in range(NBLK):
                k0 = b * KEYBLK
                part = scores[k0 : k0 + KEYBLK] + biasT[h, k0 : k0 + KEYBLK, :]
                s_scr[h, k0 : k0 + KEYBLK, :] = part
                tops[h].append(jnp.maximum(jnp.max(part, axis=0, keepdims=True), dead_score))

        def phase_weights(h):
            sums[h] = []
            for b in range(NBLK):
                k0 = b * KEYBLK
                weights = jnp.exp(s_scr[h, k0 : k0 + KEYBLK, :] - tops[h][b])
                sums[h].append(jnp.sum(weights, axis=0, keepdims=True))
                p_scr[h, k0 : k0 + KEYBLK, :] = weights.astype(BF16)

        def phase_values(h):
            low = h * WIDTH
            accs = []
            for b in range(NBLK):
                k0 = b * KEYBLK
                accs.append(
                    jnp.dot(valuesT[low : low + WIDTH, k0 : k0 + KEYBLK], p_scr[h, k0 : k0 + KEYBLK, :], preferred_element_type=F32)
                )
            top = functools.reduce(jnp.maximum, tops[h])
            factors = [jnp.exp(v - top) for v in tops[h]]
            total = sum(f * v for f, v in zip(factors, sums[h]))
            accum = sum(f * v for f, v in zip(factors, accs))
            reach = jnp.maximum(jnp.max(jnp.abs(accum), axis=0, keepdims=True), 1e-30)
            sbuf[i, low : low + WIDTH, :] = jnp.round(accum * (STEPS / reach)).astype(jnp.int32).astype(jnp.int16)
            sstat[i, h : h + 1, :] = top
            sstat[i, HEADS + h : HEADS + h + 1, :] = total
            sstat[i, 2 * HEADS + h : 2 * HEADS + h + 1, :] = reach * (1.0 / STEPS)

        for t in range(HEADS + 2):
            if t < HEADS:
                phase_scores(t)
            if 0 <= t - 1 < HEADS:
                phase_weights(t - 1)
            if 0 <= t - 2 < HEADS:
                phase_values(t - 2)

        at_home = diagonal & (i == r)

        @pl.when(at_home)
        def _():
            pltpu.make_async_copy(sbuf.at[i], rbuf.at[m], home_ls).start()
            pltpu.make_async_copy(sstat.at[i], rstat.at[m], stat_ls).start()

        @pl.when(jnp.logical_not(at_home))
        def _():
            remote(sbuf.at[i], rbuf.at[m], home_ss.at[i], home_rs.at[m], (i, r * 2 + e)).start()
            remote(sstat.at[i], rstat.at[m], stat_ss.at[i], stat_rs.at[m], (i, r * 2 + e)).start()

        return carry

    sstat[:, 3 * HEADS :, :] = jnp.zeros((NR, STATS - 3 * HEADS, CHUNK), F32)
    lax.fori_loop(0, NR, step, 0)

    gatesT = contract(wgT[...], own[...], 1, 1).astype(BF16).astype(F32)
    gates = 1.0 / (1.0 + jnp.exp(-gatesT))
    loads[3].wait()

    def home_arrived(k):
        is_self = diagonal & (m == k)

        @pl.when(is_self)
        def _():
            pltpu.make_async_copy(sbuf.at[k], rbuf.at[k], home_ls).wait()
            pltpu.make_async_copy(sstat.at[k], rstat.at[k], stat_ls).wait()

        @pl.when(jnp.logical_not(is_self))
        def _():
            remote(sbuf.at[k], rbuf.at[k], home_ss.at[k], home_rs.at[k], sib_dev).wait_recv()
            remote(sstat.at[k], rstat.at[k], stat_ss.at[k], stat_rs.at[k], sib_dev).wait_recv()

    def merge(group, so_far):
        out = []
        for h in range(HEADS):
            low = h * WIDTH
            tops = [rstat[k, h : h + 1, :] for k in group]
            sums = [rstat[k, HEADS + h : HEADS + h + 1, :] for k in group]
            if so_far is not None:
                tops.append(so_far[h][0])
                sums.append(so_far[h][1])
            top = functools.reduce(jnp.maximum, tops)
            factors = [jnp.exp(v - top) for v in tops]
            total = sum(f * v for f, v in zip(factors, sums))
            accum = sum(
                (f * rstat[k, 2 * HEADS + h : 2 * HEADS + h + 1, :]) * rbuf[k, low : low + WIDTH, :].astype(jnp.int32).astype(F32)
                for k, f in zip(group, factors)
            )
            if so_far is not None:
                accum = accum + factors[-1] * merged[low : low + WIDTH, :]
            out.append((top, total, accum))
        return out

    senders = [((r // NYH - a + NZ) % NZ) * NYH + (r + b) % NYH for b in range(NYH) for a in range(NZ)]
    for k in senders[:6]:
        home_arrived(k)
    early = merge(senders[:6], None)
    for h in range(HEADS):
        merged[h * WIDTH : (h + 1) * WIDTH, :] = early[h][2]
    for k in senders[6:]:
        home_arrived(k)
    gated = [
        (gates[h * WIDTH : (h + 1) * WIDTH] * (accum / total)).astype(BF16)
        for h, (top, total, accum) in enumerate(merge(senders[6:], early))
    ]
    gatedT = jnp.concatenate(gated, axis=0)
    out_ref[0] = contract(gatedT, w_out_ref[...], 0, 0).astype(BF16)

    for send in kv_sends + kv_ons + q_sends + q_ons:
        send.wait_send()
    bias_send.wait_send()

    @pl.when(jnp.logical_not(diagonal))
    def _():
        for send in t_sends:
            send.wait_send()

    for k in range(NR):
        remote(own, nbuf.at[k, e], sib_ss.at[k], sib_rs.at[k], sib_dev).wait_send()

        @pl.when(jnp.logical_not(diagonal & (m == k)))
        def _():
            remote(sbuf.at[k], rbuf.at[k], home_ss.at[k], home_rs.at[k], sib_dev).wait_send()
            remote(sstat.at[k], rstat.at[k], stat_ss.at[k], stat_rs.at[k], sib_dev).wait_send()


def local(pair_window, ln_gain, w_proj, w_out, pair_bias, chain_starts, chain_pads, residue_mask):
    vmem = pl.BlockSpec(memory_space=pltpu.VMEM)
    smem = pl.BlockSpec(memory_space=pltpu.SMEM)
    hbm = pl.BlockSpec(memory_space=pl.ANY)
    dma = pltpu.SemaphoreType.DMA
    return pl.pallas_call(
        kernel,
        out_shape=jax.ShapeDtypeStruct((1, CHUNK, CH), BF16),
        in_specs=[smem, smem] + [hbm] * 6,
        out_specs=vmem,
        scratch_shapes=[
            pltpu.VMEM((1, CHUNK, CH), BF16),
            pltpu.VMEM((1, CH), F32),
            pltpu.VMEM((CH, 4 * CH), BF16),
            pltpu.VMEM((CH, CH), BF16),
            pltpu.VMEM((LENGTH // KEYBLK, KEYBLK), jnp.int32),
            pltpu.VMEM((NR, 2, CHUNK, CH), BF16),
            pltpu.VMEM((NR, CHUNK, CH), BF16),
            pltpu.VMEM((2, HEADS, CHUNK, CHUNK), BF16),
            pltpu.VMEM((HEADS, KEYS, CHUNK), F32),
            pltpu.VMEM((CHUNK, CH), BF16),
            pltpu.VMEM((CH, CH), BF16),
            pltpu.VMEM((CH, CH), BF16),
            pltpu.VMEM((CH, CH), BF16),
            pltpu.VMEM((HEADS, KEYS, CHUNK), F32),
            pltpu.VMEM((HEADS, KEYS, CHUNK), BF16),
            pltpu.VMEM((NR, CH, CHUNK), jnp.int16),
            pltpu.VMEM((NR, STATS, CHUNK), F32),
            pltpu.VMEM((NM, CH, CHUNK), jnp.int16),
            pltpu.VMEM((NM, STATS, CHUNK), F32),
            pltpu.VMEM((CH, CHUNK), F32),
            dma((5,)), dma((7,)), dma((NR,)), dma((NR,)), dma((NR,)), dma((2, 7)), dma((2, NR)), dma((2,)), dma, dma, dma,
            dma((NR,)), dma((NM,)), dma, dma((NR,)), dma((NM,)), dma,
        ],
        compiler_params=pltpu.CompilerParams(
            collective_id=0, has_side_effects=True, vmem_limit_bytes=60 * 2**20
        ),
        name="triangle",
    )(
        chain_starts, chain_pads, pair_window, ln_gain.reshape(1, CH), w_proj, w_out,
        residue_mask.reshape(LENGTH // KEYBLK, KEYBLK), pair_bias,
    )


def solution(mesh):
    in_specs = (P("row", "key", None), P(), P(), P(), P(None, "row", "key"), P(), P(), P())
    out_specs = P("row", "key", None)
    return jax.shard_map(local, mesh=mesh, in_specs=in_specs, out_specs=out_specs, check_vma=False)
```

```python
import functools

import jax
import jax.numpy as jnp
from jax import lax
from jax.experimental import pallas as pl
from jax.experimental.pallas import tpu as pltpu
from jax.sharding import PartitionSpec as P

HEADS = 4
KEYBLK = 128
WIDTH = 32
CH = 128
CHUNK = 256
KEYS = 2 * CHUNK
NBLK = KEYS // KEYBLK
NX, NYL, NZ, NYH = 4, 2, 4, 2
NR = NX * NYL
NM = NZ * NYH
NCHAIN = 4
LENGTH = 4096
STATS = 2 * HEADS
STEPS = 32767.0
MESH = pl.DeviceIdType.MESH
F32 = jnp.float32
BF16 = jnp.bfloat16

epsilon = 1e-05
dead_score = -1000000000.0
dead_bias = -1e30


def contract(a, b, dim_a, dim_b):
    return lax.dot_general(a, b, (((dim_a,), (dim_b,)), ((), ())), preferred_element_type=F32)


def kernel(
    starts_ref, pads_ref, x_hbm, gain_hbm, w_hbm, w_out_hbm, mask_hbm, bias_ref, out_ref,
    x_ref, gain_ref, w_ref, w_out_ref, mask_ref,
    nbuf, qbuf, braw, biasT, own, wqT, wvT, wgT, s_scr, p_scr, sbuf, sstat, rbuf, rstat, merged,
    in_sem, kv_ss, kv_rs, sib_ss, sib_rs, q_ss, q_rs, t_ss, bias_ss, bias_rs, bias_ls, home_ss, home_rs, home_ls,
    stat_ss, stat_rs, stat_ls,
):
    r = lax.axis_index("row")
    c = lax.axis_index("key")
    m = c // 2
    e = c % 2
    x, yl = r % NX, r // NX
    z, yh = m // NYH, m % NYH
    row_at = lambda a, b: ((yl + b) % NYL) * NX + (x + a) % NX
    key_at = lambda a, b: ((z + a) % NZ) * NYH + (yh + b) % NYH
    row_dev = lambda a, b: (row_at(a, b), c)
    key_dev = lambda a, b: (r, key_at(a, b) * 2 + e)
    sib_dev = (r, m * 2 + 1 - e)
    diagonal = r == m

    def remote(src, dst, ss, rs, device):
        return pltpu.make_async_remote_copy(
            src_ref=src, dst_ref=dst, send_sem=ss, recv_sem=rs, device_id=device, device_id_type=MESH
        )

    loads = [
        pltpu.make_async_copy(src, dst, in_sem.at[n])
        for n, (src, dst) in enumerate(
            ((x_hbm, x_ref), (gain_hbm, gain_ref), (w_hbm, w_ref), (w_out_hbm, w_out_ref), (mask_hbm, mask_ref))
        )
    ]
    loads[0].start()
    loads[1].start()
    local_bias = pltpu.make_async_copy(bias_ref.at[:, pl.ds(pl.multiple_of(e * CHUNK, CHUNK), CHUNK), :], braw.at[e], bias_ls)

    barrier = pltpu.get_barrier_semaphore()
    pl.semaphore_signal(barrier, inc=1, device_id=sib_dev, device_id_type=MESH)
    for a, b in ((1, 0), (2, 0), (3, 0), (0, 1)):
        pl.semaphore_signal(barrier, inc=1, device_id=row_dev(a, b), device_id_type=MESH)
        pl.semaphore_signal(barrier, inc=1, device_id=key_dev(a, b), device_id_type=MESH)
    for k in range(NM):
        @pl.when(jnp.logical_not(diagonal & (m == k)))
        def _():
            pl.semaphore_signal(barrier, inc=1, device_id=(m, k * 2 + e), device_id_type=MESH)

    for load in loads[2:] + [local_bias]:
        load.start()

    loads[0].wait()
    loads[1].wait()
    values = x_ref[0].astype(F32)
    average = jnp.mean(values, axis=-1, keepdims=True)
    centred = values - average
    variance = jnp.mean(centred * centred, axis=-1, keepdims=True)
    normed = (centred * lax.rsqrt(variance + epsilon) * gain_ref[...]).astype(BF16)
    own[...] = normed
    nbuf[r, e] = normed

    pl.semaphore_wait(barrier, 9 + jnp.where(diagonal, NR - 1, NR))

    HALF = CHUNK // 2
    halves = [pl.ds(n * HALF, HALF) for n in range(2)]
    t_sends = [remote(own.at[v], qbuf.at[r, v], t_ss.at[n], q_rs.at[n, r], (m, r * 2 + e)) for n, v in enumerate(halves)]

    @pl.when(jnp.logical_not(diagonal))
    def _():
        for send in t_sends:
            send.start()

    @pl.when(diagonal)
    def _():
        qbuf[r] = own[...]

    partner = row_at(0, 1)
    kv_sends = [remote(own, nbuf.at[r, e], kv_ss.at[0], kv_rs.at[r], row_dev(0, 1))]
    kv_sends += [remote(own, nbuf.at[r, e], kv_ss.at[a], kv_rs.at[r], row_dev(a, 0)) for a in (1, 3, 2)]
    for send in kv_sends:
        send.start()
    remote(own, nbuf.at[r, e], sib_ss.at[r], sib_rs.at[r], sib_dev).start()
    bias_send = remote(
        bias_ref.at[:, pl.ds(pl.multiple_of((1 - e) * CHUNK, CHUNK), CHUNK), :], braw.at[e], bias_ss, bias_rs, sib_dev
    )
    bias_send.start()

    def arrived(i):
        remote(own, nbuf.at[i, e], kv_ss.at[0], kv_rs.at[i], sib_dev).wait_recv()

    def to_sibling(i):
        arrived(i)
        remote(nbuf.at[i, e], nbuf.at[i, e], sib_ss.at[i], sib_rs.at[i], sib_dev).start()

    loads[2].wait()
    for ref, low in ((wqT, 0), (wvT, 2 * CH), (wgT, 3 * CH)):
        ref[...] = w_ref[:, low : low + CH].astype(F32).T.astype(BF16)
    loads[4].wait()

    def turn_bias(core):
        for b in range(2):
            key0 = m * KEYS + core * CHUNK + b * KEYBLK
            place = key0 + lax.broadcasted_iota(jnp.int32, (1, KEYBLK), 1)
            inside = jnp.zeros((1, KEYBLK), jnp.bool_)
            leading = jnp.zeros((1, KEYBLK), jnp.bool_)
            for n in range(NCHAIN):
                start = starts_ref[n]
                end = (starts_ref[n + 1] if n < NCHAIN - 1 else LENGTH) - pads_ref[n]
                inside = inside | ((place >= start) & (place < end))
                leading = leading | (place == start)
            alive = inside & ((mask_ref[pl.ds(m * NBLK + core * 2 + b, 1), :] == 1) | leading)
            for h in range(HEADS):
                piece = braw[core, h, :, b * KEYBLK : (b + 1) * KEYBLK].astype(F32)
                piece = jnp.where(alive, piece, dead_bias)
                biasT[h, pl.ds(pl.multiple_of(core * CHUNK + b * KEYBLK, KEYBLK), KEYBLK), :] = piece.T

    local_bias.wait()
    turn_bias(e)

    arrived(partner)
    kv_ons = [remote(nbuf.at[partner, e], nbuf.at[partner, e], kv_ss.at[3 + a], kv_rs.at[partner], row_dev(a, 0)) for a in (1, 3, 2)]
    for send in kv_ons:
        send.start()
    remote(nbuf.at[partner, e], nbuf.at[partner, e], sib_ss.at[partner], sib_rs.at[partner], sib_dev).start()

    def q_arrived(i, n):
        remote(own.at[halves[n]], qbuf.at[i, halves[n]], t_ss.at[0], q_rs.at[n, i], sib_dev).wait_recv()

    def q_copy(i, n, slot, device):
        v = qbuf.at[i, halves[n]]
        return remote(v, v, q_ss.at[n, slot], q_rs.at[n, i], device)

    q_sends = []
    for n in range(2):
        @pl.when(jnp.logical_not(diagonal))
        def _():
            q_arrived(m, n)

        now = [q_copy(m, n, 0, key_dev(0, 1))] + [q_copy(m, n, a, key_dev(a, 0)) for a in (1, 3, 2)]
        for send in now:
            send.start()
        q_sends += now
    bias_send.wait_recv()
    turn_bias(1 - e)
    for a, b in ((1, 0), (3, 0), (2, 0), (1, 1), (3, 1), (2, 1)):
        to_sibling(row_at(a, b))

    other = key_at(0, 1)
    q_ons = []
    for n in range(2):
        q_arrived(other, n)
        now = [q_copy(other, n, 3 + a, key_dev(a, 0)) for a in (1, 3, 2)]
        for send in now:
            send.start()
        q_ons += now

    def turn(s):
        return ((z + s) % NZ) * NYH + (yh + s // NZ) % NYH

    def step(s, carry):
        i = turn(s)

        remote(own, nbuf.at[i, 1 - e], kv_ss.at[0], sib_rs.at[i], sib_dev).wait_recv()

        @pl.when((s > 0) & (s != NZ))
        def _():
            q_arrived(i, 0)
            q_arrived(i, 1)

        rows = nbuf[i].reshape(KEYS, CH)
        keys = jnp.dot(rows, w_ref[:, CH : 2 * CH], preferred_element_type=F32).astype(BF16)
        valuesT = contract(wvT[...], rows, 1, 1).astype(BF16)
        queriesT = (contract(wqT[...], qbuf[i], 1, 1) * (WIDTH**-0.5)).astype(BF16)
        tops, sums = {}, {}

        def phase_scores(h):
            low = h * WIDTH
            parts = []
            if low:
                parts.append(jnp.zeros((low, CHUNK), BF16))
            parts.append(queriesT[low : low + WIDTH])
            if low + WIDTH < CH:
                parts.append(jnp.zeros((CH - low - WIDTH, CHUNK), BF16))
            one_head = jnp.concatenate(parts, axis=0)
            scores = jnp.dot(keys, one_head, preferred_element_type=F32)
            tops[h] = []
            for b in range(NBLK):
                k0 = b * KEYBLK
                part = scores[k0 : k0 + KEYBLK] + biasT[h, k0 : k0 + KEYBLK, :]
                s_scr[h, k0 : k0 + KEYBLK, :] = part
                tops[h].append(jnp.maximum(jnp.max(part, axis=0, keepdims=True), dead_score))

        def phase_weights(h):
            sums[h] = []
            for b in range(NBLK):
                k0 = b * KEYBLK
                weights = jnp.exp(s_scr[h, k0 : k0 + KEYBLK, :] - tops[h][b])
                sums[h].append(jnp.sum(weights, axis=0, keepdims=True))
                p_scr[h, k0 : k0 + KEYBLK, :] = weights.astype(BF16)

        def phase_values(h):
            low = h * WIDTH
            accs = []
            for b in range(NBLK):
                k0 = b * KEYBLK
                accs.append(
                    jnp.dot(valuesT[low : low + WIDTH, k0 : k0 + KEYBLK], p_scr[h, k0 : k0 + KEYBLK, :], preferred_element_type=F32)
                )
            top = functools.reduce(jnp.maximum, tops[h])
            factors = [jnp.exp(v - top) for v in tops[h]]
            total = sum(f * v for f, v in zip(factors, sums[h]))
            accum = sum(f * v for f, v in zip(factors, accs))
            reach = jnp.maximum(jnp.max(jnp.abs(accum), axis=0, keepdims=True), 1e-30)
            sbuf[i, low : low + WIDTH, :] = jnp.round(accum * (STEPS / reach)).astype(jnp.int32).astype(jnp.int16)
            total = jnp.maximum(total, 1e-30)
            sstat[i, h : h + 1, :] = top + jnp.log(total)
            sstat[i, HEADS + h : HEADS + h + 1, :] = reach / (STEPS * total)

        for t in range(HEADS + 2):
            if t < HEADS:
                phase_scores(t)
            if 0 <= t - 1 < HEADS:
                phase_weights(t - 1)
            if 0 <= t - 2 < HEADS:
                phase_values(t - 2)

        at_home = diagonal & (i == r)

        @pl.when(at_home)
        def _():
            pltpu.make_async_copy(sbuf.at[i], rbuf.at[m], home_ls).start()
            pltpu.make_async_copy(sstat.at[i], rstat.at[m], stat_ls).start()

        @pl.when(jnp.logical_not(at_home))
        def _():
            remote(sbuf.at[i], rbuf.at[m], home_ss.at[i], home_rs.at[m], (i, r * 2 + e)).start()
            remote(sstat.at[i], rstat.at[m], stat_ss.at[i], stat_rs.at[m], (i, r * 2 + e)).start()

        return carry

    lax.fori_loop(0, NR, step, 0)

    gatesT = contract(wgT[...], own[...], 1, 1).astype(BF16).astype(F32)
    gates = 1.0 / (1.0 + jnp.exp(-gatesT))
    loads[3].wait()

    def home_arrived(k):
        is_self = diagonal & (m == k)

        @pl.when(is_self)
        def _():
            pltpu.make_async_copy(sbuf.at[k], rbuf.at[k], home_ls).wait()
            pltpu.make_async_copy(sstat.at[k], rstat.at[k], stat_ls).wait()

        @pl.when(jnp.logical_not(is_self))
        def _():
            remote(sbuf.at[k], rbuf.at[k], home_ss.at[k], home_rs.at[k], sib_dev).wait_recv()
            remote(sstat.at[k], rstat.at[k], stat_ss.at[k], stat_rs.at[k], sib_dev).wait_recv()

    def merge(group, so_far):
        out = []
        for h in range(HEADS):
            low = h * WIDTH
            tops = [rstat[k, h : h + 1, :] for k in group]
            if so_far is not None:
                tops.append(so_far[h][0])
            top = functools.reduce(jnp.maximum, tops)
            factors = [jnp.exp(v - top) for v in tops]
            total = sum(factors[: len(group)])
            if so_far is not None:
                total = total + factors[-1] * so_far[h][1]
            accum = sum(
                (f * rstat[k, HEADS + h : HEADS + h + 1, :]) * rbuf[k, low : low + WIDTH, :].astype(jnp.int32).astype(F32)
                for k, f in zip(group, factors)
            )
            if so_far is not None:
                accum = accum + factors[-1] * merged[low : low + WIDTH, :]
            out.append((top, total, accum))
        return out

    senders = [((r // NYH - a + NZ) % NZ) * NYH + (r + b) % NYH for b in range(NYH) for a in range(NZ)]
    for k in senders[:6]:
        home_arrived(k)
    early = merge(senders[:6], None)
    for h in range(HEADS):
        merged[h * WIDTH : (h + 1) * WIDTH, :] = early[h][2]
    for k in senders[6:]:
        home_arrived(k)
    gated = [
        (gates[h * WIDTH : (h + 1) * WIDTH] * (accum / total)).astype(BF16)
        for h, (top, total, accum) in enumerate(merge(senders[6:], early))
    ]
    gatedT = jnp.concatenate(gated, axis=0)
    out_ref[0] = contract(gatedT, w_out_ref[...], 0, 0).astype(BF16)

    for send in kv_sends + kv_ons + q_sends + q_ons:
        send.wait_send()
    bias_send.wait_send()

    @pl.when(jnp.logical_not(diagonal))
    def _():
        for send in t_sends:
            send.wait_send()

    for k in range(NR):
        remote(own, nbuf.at[k, e], sib_ss.at[k], sib_rs.at[k], sib_dev).wait_send()

        @pl.when(jnp.logical_not(diagonal & (m == k)))
        def _():
            remote(sbuf.at[k], rbuf.at[k], home_ss.at[k], home_rs.at[k], sib_dev).wait_send()
            remote(sstat.at[k], rstat.at[k], stat_ss.at[k], stat_rs.at[k], sib_dev).wait_send()


def local(pair_window, ln_gain, w_proj, w_out, pair_bias, chain_starts, chain_pads, residue_mask):
    vmem = pl.BlockSpec(memory_space=pltpu.VMEM)
    smem = pl.BlockSpec(memory_space=pltpu.SMEM)
    hbm = pl.BlockSpec(memory_space=pl.ANY)
    dma = pltpu.SemaphoreType.DMA
    return pl.pallas_call(
        kernel,
        out_shape=pltpu.VMEM((1, CHUNK, CH), BF16),
        in_specs=[smem, smem] + [hbm] * 6,
        out_specs=vmem,
        scratch_shapes=[
            pltpu.VMEM((1, CHUNK, CH), BF16),
            pltpu.VMEM((1, CH), F32),
            pltpu.VMEM((CH, 4 * CH), BF16),
            pltpu.VMEM((CH, CH), BF16),
            pltpu.VMEM((LENGTH // KEYBLK, KEYBLK), jnp.int32),
            pltpu.VMEM((NR, 2, CHUNK, CH), BF16),
            pltpu.VMEM((NR, CHUNK, CH), BF16),
            pltpu.VMEM((2, HEADS, CHUNK, CHUNK), BF16),
            pltpu.VMEM((HEADS, KEYS, CHUNK), F32),
            pltpu.VMEM((CHUNK, CH), BF16),
            pltpu.VMEM((CH, CH), BF16),
            pltpu.VMEM((CH, CH), BF16),
            pltpu.VMEM((CH, CH), BF16),
            pltpu.VMEM((HEADS, KEYS, CHUNK), F32),
            pltpu.VMEM((HEADS, KEYS, CHUNK), BF16),
            pltpu.VMEM((NR, CH, CHUNK), jnp.int16),
            pltpu.VMEM((NR, STATS, CHUNK), F32),
            pltpu.VMEM((NM, CH, CHUNK), jnp.int16),
            pltpu.VMEM((NM, STATS, CHUNK), F32),
            pltpu.VMEM((CH, CHUNK), F32),
            dma((5,)), dma((7,)), dma((NR,)), dma((NR,)), dma((NR,)), dma((2, 7)), dma((2, NR)), dma((2,)), dma, dma, dma,
            dma((NR,)), dma((NM,)), dma, dma((NR,)), dma((NM,)), dma,
        ],
        compiler_params=pltpu.CompilerParams(
            collective_id=0, has_side_effects=True, vmem_limit_bytes=60 * 2**20
        ),
        name="triangle",
    )(
        chain_starts, chain_pads, pair_window, ln_gain.reshape(1, CH), w_proj, w_out,
        residue_mask.reshape(LENGTH // KEYBLK, KEYBLK), pair_bias,
    )


def solution(mesh):
    in_specs = (P("row", "key", None), P(), P(), P(), P(None, "row", "key"), P(), P(), P())
    out_specs = P("row", "key", None)
    return jax.shard_map(local, mesh=mesh, in_specs=in_specs, out_specs=out_specs, check_vma=False)
```

```python
import functools

import jax
import jax.numpy as jnp
from jax import lax
from jax.experimental import pallas as pl
from jax.experimental.pallas import tpu as pltpu
from jax.sharding import PartitionSpec as P

HEADS = 4
KEYBLK = 128
WIDTH = 32
CH = 128
CHUNK = 256
KEYS = 2 * CHUNK
NBLK = KEYS // KEYBLK
NX, NYL, NZ, NYH = 4, 2, 4, 2
NR = NX * NYL
NM = NZ * NYH
NCHAIN = 4
LENGTH = 4096
STATS = 2 * HEADS
HALF = CHUNK // 2
STEPS = 32767.0
MESH = pl.DeviceIdType.MESH
F32 = jnp.float32
BF16 = jnp.bfloat16

epsilon = 1e-05
dead_score = -1000000000.0
dead_bias = -1e30


def contract(a, b, dim_a, dim_b):
    return lax.dot_general(a, b, (((dim_a,), (dim_b,)), ((), ())), preferred_element_type=F32)


def kernel(
    starts_ref, pads_ref, x_hbm, gain_hbm, w_hbm, w_out_hbm, mask_hbm, bias_ref, out_ref,
    x_ref, gain_ref, w_ref, w_out_ref, mask_ref,
    nbuf, qbuf, kbuf, vbuf, braw, biasT, own, wqT, wvT, wgT, s_scr, p_scr, sbuf, sstat, rbuf, rstat, merged,
    in_sem, kv_ss, kv_rs, sib_ss, sib_rs, q_ss, q_rs, t_ss, bias_ss, bias_rs, bias_ls, home_ss, home_rs, home_ls,
    stat_ss, stat_rs, stat_ls,
):
    r = lax.axis_index("row")
    c = lax.axis_index("key")
    m = c // 2
    e = c % 2
    x, yl = r % NX, r // NX
    z, yh = m // NYH, m % NYH
    row_at = lambda a, b: ((yl + b) % NYL) * NX + (x + a) % NX
    key_at = lambda a, b: ((z + a) % NZ) * NYH + (yh + b) % NYH
    row_dev = lambda a, b: (row_at(a, b), c)
    key_dev = lambda a, b: (r, key_at(a, b) * 2 + e)
    sib_dev = (r, m * 2 + 1 - e)
    diagonal = r == m

    def remote(src, dst, ss, rs, device):
        return pltpu.make_async_remote_copy(
            src_ref=src, dst_ref=dst, send_sem=ss, recv_sem=rs, device_id=device, device_id_type=MESH
        )

    loads = [
        pltpu.make_async_copy(src, dst, in_sem.at[n])
        for n, (src, dst) in enumerate(
            ((x_hbm, x_ref), (gain_hbm, gain_ref), (w_hbm, w_ref), (w_out_hbm, w_out_ref), (mask_hbm, mask_ref))
        )
    ]
    loads[0].start()
    loads[1].start()
    local_bias = pltpu.make_async_copy(bias_ref.at[:, pl.ds(pl.multiple_of(e * CHUNK, CHUNK), CHUNK), :], braw.at[e], bias_ls)

    barrier = pltpu.get_barrier_semaphore()
    pl.semaphore_signal(barrier, inc=1, device_id=sib_dev, device_id_type=MESH)
    for a, b in ((1, 0), (2, 0), (3, 0), (0, 1)):
        pl.semaphore_signal(barrier, inc=1, device_id=row_dev(a, b), device_id_type=MESH)
        pl.semaphore_signal(barrier, inc=1, device_id=key_dev(a, b), device_id_type=MESH)
    for k in range(NM):
        @pl.when(jnp.logical_not(diagonal & (m == k)))
        def _():
            pl.semaphore_signal(barrier, inc=1, device_id=(m, k * 2 + e), device_id_type=MESH)

    for load in loads[2:] + [local_bias]:
        load.start()

    loads[0].wait()
    loads[1].wait()
    values = x_ref[0].astype(F32)
    average = jnp.mean(values, axis=-1, keepdims=True)
    centred = values - average
    variance = jnp.mean(centred * centred, axis=-1, keepdims=True)
    normed = (centred * lax.rsqrt(variance + epsilon) * gain_ref[...]).astype(BF16)
    own[...] = normed
    nbuf[r, e] = normed

    pl.semaphore_wait(barrier, 9 + jnp.where(diagonal, NR - 1, NR))

    halves = [pl.ds(n * HALF, HALF) for n in range(2)]
    t_sends = [remote(own.at[v], qbuf.at[r, v], t_ss.at[n], q_rs.at[n, r], (m, r * 2 + e)) for n, v in enumerate(halves)]

    @pl.when(jnp.logical_not(diagonal))
    def _():
        for send in t_sends:
            send.start()

    @pl.when(diagonal)
    def _():
        qbuf[r] = own[...]

    partner = row_at(0, 1)
    kv_sends = [remote(own, nbuf.at[r, e], kv_ss.at[0], kv_rs.at[r], row_dev(0, 1))]
    kv_sends += [remote(own, nbuf.at[r, e], kv_ss.at[a], kv_rs.at[r], row_dev(a, 0)) for a in (1, 3, 2)]
    for send in kv_sends:
        send.start()
    remote(own, nbuf.at[r, e], sib_ss.at[r], sib_rs.at[r], sib_dev).start()
    bias_send = remote(
        bias_ref.at[:, pl.ds(pl.multiple_of((1 - e) * CHUNK, CHUNK), CHUNK), :], braw.at[e], bias_ss, bias_rs, sib_dev
    )
    bias_send.start()

    def arrived(i):
        remote(own, nbuf.at[i, e], kv_ss.at[0], kv_rs.at[i], sib_dev).wait_recv()

    def to_sibling(i):
        arrived(i)
        remote(nbuf.at[i, e], nbuf.at[i, e], sib_ss.at[i], sib_rs.at[i], sib_dev).start()

    loads[2].wait()
    for ref, low in ((wqT, 0), (wvT, 2 * CH), (wgT, 3 * CH)):
        ref[...] = w_ref[:, low : low + CH].astype(F32).T.astype(BF16)
    loads[4].wait()

    def turn_bias(core):
        for b in range(2):
            key0 = m * KEYS + core * CHUNK + b * KEYBLK
            place = key0 + lax.broadcasted_iota(jnp.int32, (1, KEYBLK), 1)
            inside = jnp.zeros((1, KEYBLK), jnp.bool_)
            leading = jnp.zeros((1, KEYBLK), jnp.bool_)
            for n in range(NCHAIN):
                start = starts_ref[n]
                end = (starts_ref[n + 1] if n < NCHAIN - 1 else LENGTH) - pads_ref[n]
                inside = inside | ((place >= start) & (place < end))
                leading = leading | (place == start)
            alive = inside & ((mask_ref[pl.ds(m * NBLK + core * 2 + b, 1), :] == 1) | leading)
            for h in range(HEADS):
                piece = braw[core, h, :, b * KEYBLK : (b + 1) * KEYBLK].astype(F32)
                piece = jnp.where(alive, piece, dead_bias)
                turned = piece.T
                for n in range(2):
                    biasT[
                        n, h // 2, pl.ds(pl.multiple_of(core * CHUNK + b * KEYBLK, KEYBLK), KEYBLK), (h % 2) * HALF : (h % 2 + 1) * HALF
                    ] = turned[:, n * HALF : (n + 1) * HALF]

    local_bias.wait()
    turn_bias(e)

    arrived(partner)
    kv_ons = [remote(nbuf.at[partner, e], nbuf.at[partner, e], kv_ss.at[3 + a], kv_rs.at[partner], row_dev(a, 0)) for a in (1, 3, 2)]
    for send in kv_ons:
        send.start()
    remote(nbuf.at[partner, e], nbuf.at[partner, e], sib_ss.at[partner], sib_rs.at[partner], sib_dev).start()

    def q_arrived(i, n):
        remote(own.at[halves[n]], qbuf.at[i, halves[n]], t_ss.at[0], q_rs.at[n, i], sib_dev).wait_recv()

    def q_copy(i, n, slot, device):
        v = qbuf.at[i, halves[n]]
        return remote(v, v, q_ss.at[n, slot], q_rs.at[n, i], device)

    q_sends = []
    for n in range(2):
        @pl.when(jnp.logical_not(diagonal))
        def _():
            q_arrived(m, n)

        now = [q_copy(m, n, 0, key_dev(0, 1))] + [q_copy(m, n, a, key_dev(a, 0)) for a in (1, 3, 2)]
        for send in now:
            send.start()
        q_sends += now
    bias_send.wait_recv()
    turn_bias(1 - e)
    for a, b in ((1, 0), (3, 0), (2, 0), (1, 1), (3, 1), (2, 1)):
        to_sibling(row_at(a, b))

    other = key_at(0, 1)
    q_ons = []
    for n in range(2):
        q_arrived(other, n)
        now = [q_copy(other, n, 3 + a, key_dev(a, 0)) for a in (1, 3, 2)]
        for send in now:
            send.start()
        q_ons += now

    def turn(s):
        return ((z + s) % NZ) * NYH + (yh + s // NZ) % NYH

    def step(half, count, carry):
        q_half = halves[half]
        places = [2 * count + u for u in range(2)]
        rows_i = [turn(s) for s in places]

        for s, i in zip(places, rows_i):
            if half == 0:
                remote(own, nbuf.at[i, 1 - e], kv_ss.at[0], sib_rs.at[i], sib_dev).wait_recv()

            @pl.when((s > 0) & (s != NZ))
            def _():
                remote(own.at[q_half], qbuf.at[i, q_half], t_ss.at[0], q_rs.at[half, i], sib_dev).wait_recv()

        if half == 0:
            for i in rows_i:
                rows = nbuf[i].reshape(KEYS, CH)
                kbuf[i] = jnp.dot(rows, w_ref[:, CH : 2 * CH], preferred_element_type=F32).astype(BF16)
                vbuf[i] = contract(wvT[...], rows, 1, 1).astype(BF16)

        queriesT = [(contract(wqT[...], qbuf[i, q_half, :], 1, 1) * (WIDTH**-0.5)).astype(BF16) for i in rows_i]
        tops, sums = {}, {}

        def one_head(u, h):
            low = h * WIDTH
            parts = []
            if low:
                parts.append(jnp.zeros((low, HALF), BF16))
            parts.append(queriesT[u][low : low + WIDTH])
            if low + WIDTH < CH:
                parts.append(jnp.zeros((CH - low - WIDTH, HALF), BF16))
            return jnp.concatenate(parts, axis=0)

        def phase_scores(unit):
            u, pair = unit // 2, unit % 2
            both = jnp.concatenate([one_head(u, 2 * pair), one_head(u, 2 * pair + 1)], axis=1)
            scores = jnp.dot(kbuf[rows_i[u]], both, preferred_element_type=F32)
            tops[unit] = []
            for b in range(NBLK):
                k0 = b * KEYBLK
                part = scores[k0 : k0 + KEYBLK] + biasT[half, pair, k0 : k0 + KEYBLK, :]
                s_scr[unit, k0 : k0 + KEYBLK, :] = part
                tops[unit].append(jnp.maximum(jnp.max(part, axis=0, keepdims=True), dead_score))

        def phase_weights(unit):
            sums[unit] = []
            for b in range(NBLK):
                k0 = b * KEYBLK
                weights = jnp.exp(s_scr[unit, k0 : k0 + KEYBLK, :] - tops[unit][b])
                sums[unit].append(jnp.sum(weights, axis=0, keepdims=True))
                p_scr[unit, k0 : k0 + KEYBLK, :] = weights.astype(BF16)

        def phase_values(unit):
            u, pair = unit // 2, unit % 2
            i = rows_i[u]
            low = 2 * pair * WIDTH
            accs = []
            for b in range(NBLK):
                k0 = b * KEYBLK
                both = jnp.dot(
                    vbuf[i, low : low + 2 * WIDTH, k0 : k0 + KEYBLK], p_scr[unit, k0 : k0 + KEYBLK, :], preferred_element_type=F32
                )
                accs.append(jnp.concatenate([both[:WIDTH, :HALF], both[WIDTH:, HALF:]], axis=1))
            top = functools.reduce(jnp.maximum, tops[unit])
            factors = [jnp.exp(v - top) for v in tops[unit]]
            total = jnp.maximum(sum(f * v for f, v in zip(factors, sums[unit])), 1e-30)
            accum = sum(f * v for f, v in zip(factors, accs))
            reach = jnp.maximum(jnp.max(jnp.abs(accum), axis=0, keepdims=True), 1e-30)
            whole = jnp.round(accum * (STEPS / reach)).astype(jnp.int32)
            lse = top + jnp.log(total)
            scale = reach / (STEPS * total)
            for n in range(2):
                h = 2 * pair + n
                lanes = slice(n * HALF, (n + 1) * HALF)
                sbuf[half, i, h * WIDTH : (h + 1) * WIDTH, :] = whole[:, lanes].astype(jnp.int16)
                sstat[half, i, h : h + 1, :] = lse[:, lanes]
                sstat[half, i, HEADS + h : HEADS + h + 1, :] = scale[:, lanes]

        for t in range(HEADS + 2):
            if t < HEADS:
                phase_scores(t)
            if 0 <= t - 1 < HEADS:
                phase_weights(t - 1)
            if 0 <= t - 2 < HEADS:
                phase_values(t - 2)

        for i in rows_i:
            at_home = diagonal & (i == r)

            @pl.when(at_home)
            def _():
                pltpu.make_async_copy(sbuf.at[half, i], rbuf.at[half, m], home_ls.at[half]).start()
                pltpu.make_async_copy(sstat.at[half, i], rstat.at[half, m], stat_ls.at[half]).start()

            @pl.when(jnp.logical_not(at_home))
            def _():
                remote(sbuf.at[half, i], rbuf.at[half, m], home_ss.at[half, i], home_rs.at[half, m], (i, r * 2 + e)).start()
                remote(sstat.at[half, i], rstat.at[half, m], stat_ss.at[half, i], stat_rs.at[half, m], (i, r * 2 + e)).start()

        return carry

    for half in range(2):
        lax.fori_loop(0, NR // 2, functools.partial(step, half), 0)

    gatesT = contract(wgT[...], own[...], 1, 1).astype(BF16).astype(F32)
    gates = 1.0 / (1.0 + jnp.exp(-gatesT))
    loads[3].wait()

    def home_arrived(half, k):
        is_self = diagonal & (m == k)

        @pl.when(is_self)
        def _():
            pltpu.make_async_copy(sbuf.at[half, k], rbuf.at[half, k], home_ls.at[half]).wait()
            pltpu.make_async_copy(sstat.at[half, k], rstat.at[half, k], stat_ls.at[half]).wait()

        @pl.when(jnp.logical_not(is_self))
        def _():
            remote(sbuf.at[half, k], rbuf.at[half, k], home_ss.at[half, k], home_rs.at[half, k], sib_dev).wait_recv()
            remote(sstat.at[half, k], rstat.at[half, k], stat_ss.at[half, k], stat_rs.at[half, k], sib_dev).wait_recv()

    def merge(half, group, so_far):
        out = []
        for h in range(HEADS):
            low = h * WIDTH
            tops = [rstat[half, k, h : h + 1, :] for k in group]
            if so_far is not None:
                tops.append(so_far[h][0])
            top = functools.reduce(jnp.maximum, tops)
            factors = [jnp.exp(v - top) for v in tops]
            total = sum(factors[: len(group)])
            if so_far is not None:
                total = total + factors[-1] * so_far[h][1]
            accum = sum(
                (f * rstat[half, k, HEADS + h : HEADS + h + 1, :]) * rbuf[half, k, low : low + WIDTH, :].astype(jnp.int32).astype(F32)
                for k, f in zip(group, factors)
            )
            if so_far is not None:
                accum = accum + factors[-1] * merged[low : low + WIDTH, :]
            out.append((top, total, accum))
        return out

    senders = [((r // NYH - a + NZ) % NZ) * NYH + (r + b) % NYH for b in range(NYH) for a in range(NZ)]
    for half in range(2):
        for k in senders[:6]:
            home_arrived(half, k)
        begun = merge(half, senders[:6], None)
        for h in range(HEADS):
            merged[h * WIDTH : (h + 1) * WIDTH, :] = begun[h][2]
        for k in senders[6:]:
            home_arrived(half, k)
        gated = [
            (gates[h * WIDTH : (h + 1) * WIDTH, half * HALF : (half + 1) * HALF] * (accum / total)).astype(BF16)
            for h, (top, total, accum) in enumerate(merge(half, senders[6:], begun))
        ]
        gatedT = jnp.concatenate(gated, axis=0)
        out_ref[0, half * HALF : (half + 1) * HALF, :] = contract(gatedT, w_out_ref[...], 0, 0).astype(BF16)

    for send in kv_sends + kv_ons + q_sends + q_ons:
        send.wait_send()
    bias_send.wait_send()

    @pl.when(jnp.logical_not(diagonal))
    def _():
        for send in t_sends:
            send.wait_send()

    for k in range(NR):
        remote(own, nbuf.at[k, e], sib_ss.at[k], sib_rs.at[k], sib_dev).wait_send()

        @pl.when(jnp.logical_not(diagonal & (m == k)))
        def _():
            for half in range(2):
                remote(sbuf.at[half, k], rbuf.at[half, k], home_ss.at[half, k], home_rs.at[half, k], sib_dev).wait_send()
                remote(sstat.at[half, k], rstat.at[half, k], stat_ss.at[half, k], stat_rs.at[half, k], sib_dev).wait_send()


def local(pair_window, ln_gain, w_proj, w_out, pair_bias, chain_starts, chain_pads, residue_mask):
    vmem = pl.BlockSpec(memory_space=pltpu.VMEM)
    smem = pl.BlockSpec(memory_space=pltpu.SMEM)
    hbm = pl.BlockSpec(memory_space=pl.ANY)
    dma = pltpu.SemaphoreType.DMA
    return pl.pallas_call(
        kernel,
        out_shape=pltpu.VMEM((1, CHUNK, CH), BF16),
        in_specs=[smem, smem] + [hbm] * 6,
        out_specs=vmem,
        scratch_shapes=[
            pltpu.VMEM((1, CHUNK, CH), BF16),
            pltpu.VMEM((1, CH), F32),
            pltpu.VMEM((CH, 4 * CH), BF16),
            pltpu.VMEM((CH, CH), BF16),
            pltpu.VMEM((LENGTH // KEYBLK, KEYBLK), jnp.int32),
            pltpu.VMEM((NR, 2, CHUNK, CH), BF16),
            pltpu.VMEM((NR, CHUNK, CH), BF16),
            pltpu.VMEM((NR, KEYS, CH), BF16),
            pltpu.VMEM((NR, CH, KEYS), BF16),
            pltpu.VMEM((2, HEADS, CHUNK, CHUNK), BF16),
            pltpu.VMEM((2, HEADS // 2, KEYS, CHUNK), F32),
            pltpu.VMEM((CHUNK, CH), BF16),
            pltpu.VMEM((CH, CH), BF16),
            pltpu.VMEM((CH, CH), BF16),
            pltpu.VMEM((CH, CH), BF16),
            pltpu.VMEM((HEADS, KEYS, CHUNK), F32),
            pltpu.VMEM((HEADS, KEYS, CHUNK), BF16),
            pltpu.VMEM((2, NR, CH, HALF), jnp.int16),
            pltpu.VMEM((2, NR, STATS, HALF), F32),
            pltpu.VMEM((2, NM, CH, HALF), jnp.int16),
            pltpu.VMEM((2, NM, STATS, HALF), F32),
            pltpu.VMEM((CH, HALF), F32),
            dma((5,)), dma((7,)), dma((NR,)), dma((NR,)), dma((NR,)), dma((2, 7)), dma((2, NR)), dma((2,)), dma, dma, dma,
            dma((2, NR)), dma((2, NM)), dma((2,)), dma((2, NR)), dma((2, NM)), dma((2,)),
        ],
        compiler_params=pltpu.CompilerParams(
            collective_id=0, has_side_effects=True, vmem_limit_bytes=60 * 2**20
        ),
        name="triangle",
    )(
        chain_starts, chain_pads, pair_window, ln_gain.reshape(1, CH), w_proj, w_out,
        residue_mask.reshape(LENGTH // KEYBLK, KEYBLK), pair_bias,
    )


def solution(mesh):
    in_specs = (P("row", "key", None), P(), P(), P(), P(None, "row", "key"), P(), P(), P())
    out_specs = P("row", "key", None)
    return jax.shard_map(local, mesh=mesh, in_specs=in_specs, out_specs=out_specs, check_vma=False)
```

```python
import functools

import jax
import jax.numpy as jnp
from jax import lax
from jax.experimental import pallas as pl
from jax.experimental.pallas import tpu as pltpu
from jax.sharding import PartitionSpec as P

HEADS = 4
KEYBLK = 128
WIDTH = 32
CH = 128
CHUNK = 256
KEYS = 2 * CHUNK
NBLK = KEYS // KEYBLK
NX, NYL, NZ, NYH = 4, 2, 4, 2
NR = NX * NYL
NM = NZ * NYH
NCHAIN = 4
LENGTH = 4096
STATS = 2 * HEADS
HALF = CHUNK // 2
STEPS = 32767.0
MESH = pl.DeviceIdType.MESH
F32 = jnp.float32
BF16 = jnp.bfloat16

epsilon = 1e-05
dead_score = -1000000000.0
dead_bias = -1e30


def contract(a, b, dim_a, dim_b):
    return lax.dot_general(a, b, (((dim_a,), (dim_b,)), ((), ())), preferred_element_type=F32)


def kernel(
    starts_ref, pads_ref, x_hbm, gain_hbm, w_hbm, w_out_hbm, mask_hbm, bias_ref, out_ref,
    x_ref, gain_ref, w_ref, w_out_ref, mask_ref,
    nbuf, qbuf, kbuf, vbuf, braw, biasT, own, wqT, wvT, wgT, s_scr, p_scr, sbuf, sstat, rbuf, rstat, merged,
    in_sem, kv_ss, kv_rs, sib_ss, sib_rs, q_ss, q_rs, t_ss, bias_ss, bias_rs, bias_ls, home_ss, home_rs, home_ls,
    stat_ss, stat_rs, stat_ls,
):
    r = lax.axis_index("row")
    c = lax.axis_index("key")
    m = c // 2
    e = c % 2
    x, yl = r % NX, r // NX
    z, yh = m // NYH, m % NYH
    row_at = lambda a, b: ((yl + b) % NYL) * NX + (x + a) % NX
    key_at = lambda a, b: ((z + a) % NZ) * NYH + (yh + b) % NYH
    row_dev = lambda a, b: (row_at(a, b), c)
    key_dev = lambda a, b: (r, key_at(a, b) * 2 + e)
    sib_dev = (r, m * 2 + 1 - e)
    diagonal = r == m

    def remote(src, dst, ss, rs, device):
        return pltpu.make_async_remote_copy(
            src_ref=src, dst_ref=dst, send_sem=ss, recv_sem=rs, device_id=device, device_id_type=MESH
        )

    loads = [
        pltpu.make_async_copy(src, dst, in_sem.at[n])
        for n, (src, dst) in enumerate(
            ((x_hbm, x_ref), (gain_hbm, gain_ref), (w_hbm, w_ref), (w_out_hbm, w_out_ref), (mask_hbm, mask_ref))
        )
    ]
    loads[0].start()
    loads[1].start()
    local_bias = pltpu.make_async_copy(bias_ref.at[:, pl.ds(pl.multiple_of(e * CHUNK, CHUNK), CHUNK), :], braw.at[e], bias_ls)

    barrier = pltpu.get_barrier_semaphore()
    pl.semaphore_signal(barrier, inc=1, device_id=sib_dev, device_id_type=MESH)
    for a, b in ((1, 0), (2, 0), (3, 0), (0, 1)):
        pl.semaphore_signal(barrier, inc=1, device_id=row_dev(a, b), device_id_type=MESH)
        pl.semaphore_signal(barrier, inc=1, device_id=key_dev(a, b), device_id_type=MESH)
    for k in range(NM):
        @pl.when(jnp.logical_not(diagonal & (m == k)))
        def _():
            pl.semaphore_signal(barrier, inc=1, device_id=(m, k * 2 + e), device_id_type=MESH)

    for load in loads[2:] + [local_bias]:
        load.start()

    loads[0].wait()
    loads[1].wait()
    values = x_ref[0].astype(F32)
    average = jnp.mean(values, axis=-1, keepdims=True)
    centred = values - average
    variance = jnp.mean(centred * centred, axis=-1, keepdims=True)
    normed = (centred * lax.rsqrt(variance + epsilon) * gain_ref[...]).astype(BF16)
    own[...] = normed
    nbuf[r, e] = normed

    pl.semaphore_wait(barrier, 9 + jnp.where(diagonal, NR - 1, NR))

    halves = [pl.ds(n * HALF, HALF) for n in range(2)]
    t_sends = [remote(own.at[v], qbuf.at[r, v], t_ss.at[n], q_rs.at[n, r], (m, r * 2 + e)) for n, v in enumerate(halves)]

    @pl.when(jnp.logical_not(diagonal))
    def _():
        for send in t_sends:
            send.start()

    @pl.when(diagonal)
    def _():
        qbuf[r] = own[...]

    partner = row_at(0, 1)
    kv_sends = [remote(own, nbuf.at[r, e], kv_ss.at[0], kv_rs.at[r], row_dev(0, 1))]
    kv_sends += [remote(own, nbuf.at[r, e], kv_ss.at[a], kv_rs.at[r], row_dev(a, 0)) for a in (1, 3, 2)]
    for send in kv_sends:
        send.start()
    remote(own, nbuf.at[r, e], sib_ss.at[r], sib_rs.at[r], sib_dev).start()
    bias_send = remote(
        bias_ref.at[:, pl.ds(pl.multiple_of((1 - e) * CHUNK, CHUNK), CHUNK), :], braw.at[e], bias_ss, bias_rs, sib_dev
    )
    bias_send.start()

    def arrived(i):
        remote(own, nbuf.at[i, e], kv_ss.at[0], kv_rs.at[i], sib_dev).wait_recv()

    def to_sibling(i):
        arrived(i)
        remote(nbuf.at[i, e], nbuf.at[i, e], sib_ss.at[i], sib_rs.at[i], sib_dev).start()

    loads[2].wait()
    for ref, low in ((wqT, 0), (wvT, 2 * CH), (wgT, 3 * CH)):
        ref[...] = w_ref[:, low : low + CH].astype(F32).T.astype(BF16)
    loads[4].wait()

    def turn_bias(core):
        for b in range(2):
            key0 = m * KEYS + core * CHUNK + b * KEYBLK
            place = key0 + lax.broadcasted_iota(jnp.int32, (1, KEYBLK), 1)
            inside = jnp.zeros((1, KEYBLK), jnp.bool_)
            leading = jnp.zeros((1, KEYBLK), jnp.bool_)
            for n in range(NCHAIN):
                start = starts_ref[n]
                end = (starts_ref[n + 1] if n < NCHAIN - 1 else LENGTH) - pads_ref[n]
                inside = inside | ((place >= start) & (place < end))
                leading = leading | (place == start)
            alive = inside & ((mask_ref[pl.ds(m * NBLK + core * 2 + b, 1), :] == 1) | leading)
            for h in range(HEADS):
                piece = braw[core, h, :, b * KEYBLK : (b + 1) * KEYBLK].astype(F32)
                piece = jnp.where(alive, piece, dead_bias)
                turned = piece.T
                for n in range(2):
                    biasT[
                        n, h // 2, pl.ds(pl.multiple_of(core * CHUNK + b * KEYBLK, KEYBLK), KEYBLK), (h % 2) * HALF : (h % 2 + 1) * HALF
                    ] = turned[:, n * HALF : (n + 1) * HALF]

    local_bias.wait()
    turn_bias(e)

    arrived(partner)
    kv_ons = [remote(nbuf.at[partner, e], nbuf.at[partner, e], kv_ss.at[3 + a], kv_rs.at[partner], row_dev(a, 0)) for a in (1, 3, 2)]
    for send in kv_ons:
        send.start()
    remote(nbuf.at[partner, e], nbuf.at[partner, e], sib_ss.at[partner], sib_rs.at[partner], sib_dev).start()

    def q_arrived(i, n):
        remote(own.at[halves[n]], qbuf.at[i, halves[n]], t_ss.at[0], q_rs.at[n, i], sib_dev).wait_recv()

    def q_copy(i, n, slot, device):
        v = qbuf.at[i, halves[n]]
        return remote(v, v, q_ss.at[n, slot], q_rs.at[n, i], device)

    def share(n):
        @pl.when(jnp.logical_not(diagonal))
        def _():
            q_arrived(m, n)

        now = [q_copy(m, n, 0, key_dev(0, 1))] + [q_copy(m, n, a, key_dev(a, 0)) for a in (1, 3, 2)]
        for send in now:
            send.start()
        return now

    first = share(0)
    bias_send.wait_recv()
    turn_bias(1 - e)
    second = share(1)
    for a, b in ((1, 0), (3, 0), (2, 0), (1, 1), (3, 1), (2, 1)):
        to_sibling(row_at(a, b))

    other = key_at(0, 1)
    q_ons = []
    for n in range(2):
        q_arrived(other, n)
        now = [q_copy(other, n, 3 + a, key_dev(a, 0)) for a in (1, 3, 2)]
        for send in now:
            send.start()
        q_ons += now

    def turn(s):
        return ((z + s) % NZ) * NYH + (yh + s // NZ) % NYH

    def step(half, count, carry):
        q_half = halves[half]
        places = [2 * count + u for u in range(2)]
        rows_i = [turn(s) for s in places]

        for s, i in zip(places, rows_i):
            if half == 0:
                remote(own, nbuf.at[i, 1 - e], kv_ss.at[0], sib_rs.at[i], sib_dev).wait_recv()

            @pl.when((s > 0) & (s != NZ))
            def _():
                remote(own.at[q_half], qbuf.at[i, q_half], t_ss.at[0], q_rs.at[half, i], sib_dev).wait_recv()

        if half == 0:
            for i in rows_i:
                rows = nbuf[i].reshape(KEYS, CH)
                kbuf[i] = jnp.dot(rows, w_ref[:, CH : 2 * CH], preferred_element_type=F32).astype(BF16)
                vbuf[i] = contract(wvT[...], rows, 1, 1).astype(BF16)

        queriesT = [(contract(wqT[...], qbuf[i, q_half, :], 1, 1) * (WIDTH**-0.5)).astype(BF16) for i in rows_i]
        tops, sums = {}, {}

        def one_head(u, h):
            low = h * WIDTH
            parts = []
            if low:
                parts.append(jnp.zeros((low, HALF), BF16))
            parts.append(queriesT[u][low : low + WIDTH])
            if low + WIDTH < CH:
                parts.append(jnp.zeros((CH - low - WIDTH, HALF), BF16))
            return jnp.concatenate(parts, axis=0)

        def phase_scores(unit):
            u, pair = unit // 2, unit % 2
            both = jnp.concatenate([one_head(u, 2 * pair), one_head(u, 2 * pair + 1)], axis=1)
            scores = jnp.dot(kbuf[rows_i[u]], both, preferred_element_type=F32)
            tops[unit] = []
            for b in range(NBLK):
                k0 = b * KEYBLK
                part = scores[k0 : k0 + KEYBLK] + biasT[half, pair, k0 : k0 + KEYBLK, :]
                s_scr[unit, k0 : k0 + KEYBLK, :] = part
                tops[unit].append(jnp.maximum(jnp.max(part, axis=0, keepdims=True), dead_score))

        def phase_weights(unit):
            sums[unit] = []
            for b in range(NBLK):
                k0 = b * KEYBLK
                weights = jnp.exp(s_scr[unit, k0 : k0 + KEYBLK, :] - tops[unit][b])
                sums[unit].append(jnp.sum(weights.reshape(KEYBLK // 8, 8, CHUNK), axis=0))
                p_scr[unit, k0 : k0 + KEYBLK, :] = weights.astype(BF16)

        def phase_values(unit):
            u, pair = unit // 2, unit % 2
            i = rows_i[u]
            low = 2 * pair * WIDTH
            accs = []
            for b in range(NBLK):
                k0 = b * KEYBLK
                both = jnp.dot(
                    vbuf[i, low : low + 2 * WIDTH, k0 : k0 + KEYBLK], p_scr[unit, k0 : k0 + KEYBLK, :], preferred_element_type=F32
                )
                accs.append(jnp.concatenate([both[:WIDTH, :HALF], both[WIDTH:, HALF:]], axis=1))
            top = functools.reduce(jnp.maximum, tops[unit])
            factors = [jnp.exp(v - top) for v in tops[unit]]
            total = jnp.maximum(jnp.sum(sum(f * v for f, v in zip(factors, sums[unit])), axis=0, keepdims=True), 1e-30)
            accum = sum(f * v for f, v in zip(factors, accs))
            reach = jnp.maximum(jnp.max(jnp.abs(accum), axis=0, keepdims=True), 1e-30)
            whole = jnp.round(accum * (STEPS / reach)).astype(jnp.int32)
            lse = top + jnp.log(total)
            scale = reach / (STEPS * total)
            for n in range(2):
                h = 2 * pair + n
                lanes = slice(n * HALF, (n + 1) * HALF)
                sbuf[half, i, h * WIDTH : (h + 1) * WIDTH, :] = whole[:, lanes].astype(jnp.int16)
                sstat[half, i, h : h + 1, :] = lse[:, lanes]
                sstat[half, i, HEADS + h : HEADS + h + 1, :] = scale[:, lanes]

        phase_scores(0)
        phase_scores(1)
        phase_weights(0)
        phase_scores(2)
        phase_weights(1)
        phase_values(0)
        phase_scores(3)
        phase_weights(2)
        phase_values(1)
        phase_weights(3)
        phase_values(2)
        phase_values(3)

        for i in rows_i:
            at_home = diagonal & (i == r)

            @pl.when(at_home)
            def _():
                pltpu.make_async_copy(sbuf.at[half, i], rbuf.at[half, m], home_ls.at[half]).start()
                pltpu.make_async_copy(sstat.at[half, i], rstat.at[half, m], stat_ls.at[half]).start()

            @pl.when(jnp.logical_not(at_home))
            def _():
                remote(sbuf.at[half, i], rbuf.at[half, m], home_ss.at[half, i], home_rs.at[half, m], (i, r * 2 + e)).start()
                remote(sstat.at[half, i], rstat.at[half, m], stat_ss.at[half, i], stat_rs.at[half, m], (i, r * 2 + e)).start()

        return carry

    for half in range(2):
        lax.fori_loop(0, NR // 2, functools.partial(step, half), 0)

    gatesT = contract(wgT[...], own[...], 1, 1).astype(BF16).astype(F32)
    gates = 1.0 / (1.0 + jnp.exp(-gatesT))
    loads[3].wait()

    def home_arrived(half, k):
        is_self = diagonal & (m == k)

        @pl.when(is_self)
        def _():
            pltpu.make_async_copy(sbuf.at[half, k], rbuf.at[half, k], home_ls.at[half]).wait()
            pltpu.make_async_copy(sstat.at[half, k], rstat.at[half, k], stat_ls.at[half]).wait()

        @pl.when(jnp.logical_not(is_self))
        def _():
            remote(sbuf.at[half, k], rbuf.at[half, k], home_ss.at[half, k], home_rs.at[half, k], sib_dev).wait_recv()
            remote(sstat.at[half, k], rstat.at[half, k], stat_ss.at[half, k], stat_rs.at[half, k], sib_dev).wait_recv()

    def merge(half, group, so_far):
        out = []
        for h in range(HEADS):
            low = h * WIDTH
            tops = [rstat[half, k, h : h + 1, :] for k in group]
            if so_far is not None:
                tops.append(so_far[h][0])
            top = functools.reduce(jnp.maximum, tops)
            factors = [jnp.exp(v - top) for v in tops]
            total = sum(factors[: len(group)])
            if so_far is not None:
                total = total + factors[-1] * so_far[h][1]
            accum = sum(
                (f * rstat[half, k, HEADS + h : HEADS + h + 1, :]) * rbuf[half, k, low : low + WIDTH, :].astype(jnp.int32).astype(F32)
                for k, f in zip(group, factors)
            )
            if so_far is not None:
                accum = accum + factors[-1] * merged[low : low + WIDTH, :]
            out.append((top, total, accum))
        return out

    senders = [((r // NYH - a + NZ) % NZ) * NYH + (r + b) % NYH for b in range(NYH) for a in range(NZ)]
    for half in range(2):
        for k in senders[:6]:
            home_arrived(half, k)
        begun = merge(half, senders[:6], None)
        for h in range(HEADS):
            merged[h * WIDTH : (h + 1) * WIDTH, :] = begun[h][2]
        for k in senders[6:]:
            home_arrived(half, k)
        gated = [
            (gates[h * WIDTH : (h + 1) * WIDTH, half * HALF : (half + 1) * HALF] * (accum / total)).astype(BF16)
            for h, (top, total, accum) in enumerate(merge(half, senders[6:], begun))
        ]
        gatedT = jnp.concatenate(gated, axis=0)
        out_ref[0, half * HALF : (half + 1) * HALF, :] = contract(gatedT, w_out_ref[...], 0, 0).astype(BF16)

    for send in kv_sends + kv_ons + first + second + q_ons:
        send.wait_send()
    bias_send.wait_send()

    @pl.when(jnp.logical_not(diagonal))
    def _():
        for send in t_sends:
            send.wait_send()

    for k in range(NR):
        remote(own, nbuf.at[k, e], sib_ss.at[k], sib_rs.at[k], sib_dev).wait_send()

        @pl.when(jnp.logical_not(diagonal & (m == k)))
        def _():
            for half in range(2):
                remote(sbuf.at[half, k], rbuf.at[half, k], home_ss.at[half, k], home_rs.at[half, k], sib_dev).wait_send()
                remote(sstat.at[half, k], rstat.at[half, k], stat_ss.at[half, k], stat_rs.at[half, k], sib_dev).wait_send()


def local(pair_window, ln_gain, w_proj, w_out, pair_bias, chain_starts, chain_pads, residue_mask):
    vmem = pl.BlockSpec(memory_space=pltpu.VMEM)
    smem = pl.BlockSpec(memory_space=pltpu.SMEM)
    hbm = pl.BlockSpec(memory_space=pl.ANY)
    dma = pltpu.SemaphoreType.DMA
    return pl.pallas_call(
        kernel,
        out_shape=pltpu.VMEM((1, CHUNK, CH), BF16),
        in_specs=[smem, smem] + [hbm] * 6,
        out_specs=vmem,
        scratch_shapes=[
            pltpu.VMEM((1, CHUNK, CH), BF16),
            pltpu.VMEM((1, CH), F32),
            pltpu.VMEM((CH, 4 * CH), BF16),
            pltpu.VMEM((CH, CH), BF16),
            pltpu.VMEM((LENGTH // KEYBLK, KEYBLK), jnp.int32),
            pltpu.VMEM((NR, 2, CHUNK, CH), BF16),
            pltpu.VMEM((NR, CHUNK, CH), BF16),
            pltpu.VMEM((NR, KEYS, CH), BF16),
            pltpu.VMEM((NR, CH, KEYS), BF16),
            pltpu.VMEM((2, HEADS, CHUNK, CHUNK), BF16),
            pltpu.VMEM((2, HEADS // 2, KEYS, CHUNK), F32),
            pltpu.VMEM((CHUNK, CH), BF16),
            pltpu.VMEM((CH, CH), BF16),
            pltpu.VMEM((CH, CH), BF16),
            pltpu.VMEM((CH, CH), BF16),
            pltpu.VMEM((HEADS, KEYS, CHUNK), F32),
            pltpu.VMEM((HEADS, KEYS, CHUNK), BF16),
            pltpu.VMEM((2, NR, CH, HALF), jnp.int16),
            pltpu.VMEM((2, NR, STATS, HALF), F32),
            pltpu.VMEM((2, NM, CH, HALF), jnp.int16),
            pltpu.VMEM((2, NM, STATS, HALF), F32),
            pltpu.VMEM((CH, HALF), F32),
            dma((5,)), dma((7,)), dma((NR,)), dma((NR,)), dma((NR,)), dma((2, 7)), dma((2, NR)), dma((2,)), dma, dma, dma,
            dma((2, NR)), dma((2, NM)), dma((2,)), dma((2, NR)), dma((2, NM)), dma((2,)),
        ],
        compiler_params=pltpu.CompilerParams(
            collective_id=0, has_side_effects=True, vmem_limit_bytes=60 * 2**20
        ),
        name="triangle",
    )(
        chain_starts, chain_pads, pair_window, ln_gain.reshape(1, CH), w_proj, w_out,
        residue_mask.reshape(LENGTH // KEYBLK, KEYBLK), pair_bias,
    )


def solution(mesh):
    in_specs = (P("row", "key", None), P(), P(), P(), P(None, "row", "key"), P(), P(), P())
    out_specs = P("row", "key", None)
    return jax.shard_map(local, mesh=mesh, in_specs=in_specs, out_specs=out_specs, check_vma=False)
```

```python
import functools

import jax
import jax.numpy as jnp
from jax import lax
from jax.experimental import pallas as pl
from jax.experimental.pallas import tpu as pltpu
from jax.sharding import PartitionSpec as P

HEADS = 4
KEYBLK = 128
WIDTH = 32
CH = 128
CHUNK = 256
KEYS = 2 * CHUNK
NBLK = KEYS // KEYBLK
NX, NYL, NZ, NYH = 4, 2, 4, 2
NR = NX * NYL
NM = NZ * NYH
NCHAIN = 4
LENGTH = 4096
STATS = 2 * HEADS
HALF = CHUNK // 2
STEPS = 32767.0
MESH = pl.DeviceIdType.MESH
F32 = jnp.float32
BF16 = jnp.bfloat16

epsilon = 1e-05
dead_score = -1000000000.0
dead_bias = -1e30


def contract(a, b, dim_a, dim_b):
    return lax.dot_general(a, b, (((dim_a,), (dim_b,)), ((), ())), preferred_element_type=F32)


OTHERS = ((2, 1), (1, 1), (3, 1), (2, 0), (0, 1), (1, 0), (3, 0))


def kernel(
    starts_ref, pads_ref, x_hbm, gain_hbm, w_hbm, w_out_hbm, mask_hbm, bias_ref, out_ref,
    x_ref, gain_ref, w_ref, w_out_ref, mask_ref,
    nbuf, qbuf, kbuf, vbuf, braw, biasT, own, wqT, wvT, wgT, s_scr, p_scr, sbuf, sstat, rbuf, rstat, merged,
    in_sem, kv_ss, kv_rs, sib_ss, sib_rs, q_ss, q_rs, t_ss, bias_ss, bias_rs, bias_ls, home_ss, home_rs, home_ls,
    stat_ss, stat_rs, stat_ls,
):
    r = lax.axis_index("row")
    c = lax.axis_index("key")
    m = c // 2
    e = c % 2
    x, yl = r % NX, r // NX
    z, yh = m // NYH, m % NYH
    row_at = lambda a, b: ((yl + b) % NYL) * NX + (x + a) % NX
    key_at = lambda a, b: ((z + a) % NZ) * NYH + (yh + b) % NYH
    row_dev = lambda a, b: (row_at(a, b), c)
    key_dev = lambda a, b: (r, key_at(a, b) * 2 + e)
    sib_dev = (r, m * 2 + 1 - e)
    diagonal = r == m

    def remote(src, dst, ss, rs, device):
        return pltpu.make_async_remote_copy(
            src_ref=src, dst_ref=dst, send_sem=ss, recv_sem=rs, device_id=device, device_id_type=MESH
        )

    loads = [
        pltpu.make_async_copy(src, dst, in_sem.at[n])
        for n, (src, dst) in enumerate(
            ((x_hbm, x_ref), (gain_hbm, gain_ref), (w_hbm, w_ref), (w_out_hbm, w_out_ref), (mask_hbm, mask_ref))
        )
    ]
    loads[0].start()
    loads[1].start()
    local_bias = pltpu.make_async_copy(bias_ref.at[:, pl.ds(pl.multiple_of(e * CHUNK, CHUNK), CHUNK), :], braw.at[e], bias_ls)

    barrier = pltpu.get_barrier_semaphore()
    def greet(device):
        pl.semaphore_signal(barrier, inc=1, device_id=device, device_id_type=MESH)

    greet(sib_dev)

    @pl.when(jnp.logical_not(diagonal))
    def _():
        greet((m, r * 2 + e))

    for a, b in OTHERS:
        greet(row_dev(a, b))
        greet(key_dev(a, b))

    for load in loads[2:] + [local_bias]:
        load.start()

    loads[0].wait()
    loads[1].wait()
    values = x_ref[0].astype(F32)
    average = jnp.mean(values, axis=-1, keepdims=True)
    centred = values - average
    variance = jnp.mean(centred * centred, axis=-1, keepdims=True)
    normed = (centred * lax.rsqrt(variance + epsilon) * gain_ref[...]).astype(BF16)
    own[...] = normed
    nbuf[r, e] = normed

    pl.semaphore_wait(barrier, 15 + jnp.where(diagonal, 0, 1))

    halves = [pl.ds(n * HALF, HALF) for n in range(2)]
    t_sends = [remote(own.at[v], qbuf.at[r, v], t_ss.at[n], q_rs.at[n, r], (m, r * 2 + e)) for n, v in enumerate(halves)]

    @pl.when(jnp.logical_not(diagonal))
    def _():
        for send in t_sends:
            send.start()

    @pl.when(diagonal)
    def _():
        qbuf[r] = own[...]

    partner = row_at(0, 1)
    kv_sends = [remote(own, nbuf.at[r, e], kv_ss.at[0], kv_rs.at[r], row_dev(0, 1))]
    kv_sends += [remote(own, nbuf.at[r, e], kv_ss.at[a], kv_rs.at[r], row_dev(a, 0)) for a in (1, 3, 2)]
    for send in kv_sends:
        send.start()
    remote(own, nbuf.at[r, e], sib_ss.at[r], sib_rs.at[r], sib_dev).start()
    bias_send = remote(
        bias_ref.at[:, pl.ds(pl.multiple_of((1 - e) * CHUNK, CHUNK), CHUNK), :], braw.at[e], bias_ss, bias_rs, sib_dev
    )
    bias_send.start()

    def arrived(i):
        remote(own, nbuf.at[i, e], kv_ss.at[0], kv_rs.at[i], sib_dev).wait_recv()

    def to_sibling(i):
        arrived(i)
        remote(nbuf.at[i, e], nbuf.at[i, e], sib_ss.at[i], sib_rs.at[i], sib_dev).start()

    loads[2].wait()
    for ref, low in ((wqT, 0), (wvT, 2 * CH), (wgT, 3 * CH)):
        ref[...] = w_ref[:, low : low + CH].astype(F32).T.astype(BF16)
    loads[4].wait()

    def turn_bias(core):
        for b in range(2):
            key0 = m * KEYS + core * CHUNK + b * KEYBLK
            place = key0 + lax.broadcasted_iota(jnp.int32, (1, KEYBLK), 1)
            inside = jnp.zeros((1, KEYBLK), jnp.bool_)
            leading = jnp.zeros((1, KEYBLK), jnp.bool_)
            for n in range(NCHAIN):
                start = starts_ref[n]
                end = (starts_ref[n + 1] if n < NCHAIN - 1 else LENGTH) - pads_ref[n]
                inside = inside | ((place >= start) & (place < end))
                leading = leading | (place == start)
            alive = inside & ((mask_ref[pl.ds(m * NBLK + core * 2 + b, 1), :] == 1) | leading)
            for h in range(HEADS):
                piece = braw[core, h, :, b * KEYBLK : (b + 1) * KEYBLK].astype(F32)
                piece = jnp.where(alive, piece, dead_bias)
                turned = piece.T
                for n in range(2):
                    biasT[
                        n, h // 2, pl.ds(pl.multiple_of(core * CHUNK + b * KEYBLK, KEYBLK), KEYBLK), (h % 2) * HALF : (h % 2 + 1) * HALF
                    ] = turned[:, n * HALF : (n + 1) * HALF]

    local_bias.wait()
    turn_bias(e)

    arrived(partner)
    kv_ons = [remote(nbuf.at[partner, e], nbuf.at[partner, e], kv_ss.at[3 + a], kv_rs.at[partner], row_dev(a, 0)) for a in (1, 3, 2)]
    for send in kv_ons:
        send.start()
    remote(nbuf.at[partner, e], nbuf.at[partner, e], sib_ss.at[partner], sib_rs.at[partner], sib_dev).start()

    def q_arrived(i, n):
        remote(own.at[halves[n]], qbuf.at[i, halves[n]], t_ss.at[0], q_rs.at[n, i], sib_dev).wait_recv()

    def q_copy(i, n, slot, device):
        v = qbuf.at[i, halves[n]]
        return remote(v, v, q_ss.at[n, slot], q_rs.at[n, i], device)

    def share(n):
        @pl.when(jnp.logical_not(diagonal))
        def _():
            q_arrived(m, n)

        now = [q_copy(m, n, 0, key_dev(0, 1))] + [q_copy(m, n, a, key_dev(a, 0)) for a in (1, 3, 2)]
        for send in now:
            send.start()
        return now

    first = share(0)
    bias_send.wait_recv()
    turn_bias(1 - e)
    second = share(1)
    for a, b in ((1, 0), (3, 0), (2, 0), (1, 1), (3, 1), (2, 1)):
        to_sibling(row_at(a, b))

    other = key_at(0, 1)
    q_ons = []
    for n in range(2):
        q_arrived(other, n)
        now = [q_copy(other, n, 3 + a, key_dev(a, 0)) for a in (1, 3, 2)]
        for send in now:
            send.start()
        q_ons += now

    def turn(s):
        return ((z + s) % NZ) * NYH + (yh + s // NZ) % NYH

    def step(half, count, carry):
        q_half = halves[half]
        places = [2 * count + u for u in range(2)]
        rows_i = [turn(s) for s in places]

        for s, i in zip(places, rows_i):
            if half == 0:
                remote(own, nbuf.at[i, 1 - e], kv_ss.at[0], sib_rs.at[i], sib_dev).wait_recv()

            @pl.when((s > 0) & (s != NZ))
            def _():
                remote(own.at[q_half], qbuf.at[i, q_half], t_ss.at[0], q_rs.at[half, i], sib_dev).wait_recv()

        if half == 0:
            for i in rows_i:
                rows = nbuf[i].reshape(KEYS, CH)
                kbuf[i] = jnp.dot(rows, w_ref[:, CH : 2 * CH], preferred_element_type=F32).astype(BF16)
                vbuf[i] = contract(wvT[...], rows, 1, 1).astype(BF16)

        queriesT = [(contract(wqT[...], qbuf[i, q_half, :], 1, 1) * (WIDTH**-0.5)).astype(BF16) for i in rows_i]
        tops, sums = {}, {}

        def one_head(u, h):
            low = h * WIDTH
            parts = []
            if low:
                parts.append(jnp.zeros((low, HALF), BF16))
            parts.append(queriesT[u][low : low + WIDTH])
            if low + WIDTH < CH:
                parts.append(jnp.zeros((CH - low - WIDTH, HALF), BF16))
            return jnp.concatenate(parts, axis=0)

        def phase_scores(unit):
            u, pair = unit // 2, unit % 2
            both = jnp.concatenate([one_head(u, 2 * pair), one_head(u, 2 * pair + 1)], axis=1)
            scores = jnp.dot(kbuf[rows_i[u]], both, preferred_element_type=F32)
            tops[unit] = []
            for b in range(NBLK):
                k0 = b * KEYBLK
                part = scores[k0 : k0 + KEYBLK] + biasT[half, pair, k0 : k0 + KEYBLK, :]
                s_scr[unit, k0 : k0 + KEYBLK, :] = part
                tops[unit].append(jnp.maximum(jnp.max(part, axis=0, keepdims=True), dead_score))

        def phase_weights(unit):
            sums[unit] = []
            for b in range(NBLK):
                k0 = b * KEYBLK
                weights = jnp.exp(s_scr[unit, k0 : k0 + KEYBLK, :] - tops[unit][b])
                sums[unit].append(jnp.sum(weights.reshape(KEYBLK // 8, 8, CHUNK), axis=0))
                p_scr[unit, k0 : k0 + KEYBLK, :] = weights.astype(BF16)

        def phase_values(unit):
            u, pair = unit // 2, unit % 2
            i = rows_i[u]
            low = 2 * pair * WIDTH
            accs = []
            for b in range(NBLK):
                k0 = b * KEYBLK
                both = jnp.dot(
                    vbuf[i, low : low + 2 * WIDTH, k0 : k0 + KEYBLK], p_scr[unit, k0 : k0 + KEYBLK, :], preferred_element_type=F32
                )
                accs.append(jnp.concatenate([both[:WIDTH, :HALF], both[WIDTH:, HALF:]], axis=1))
            top = functools.reduce(jnp.maximum, tops[unit])
            factors = [jnp.exp(v - top) for v in tops[unit]]
            total = jnp.maximum(jnp.sum(sum(f * v for f, v in zip(factors, sums[unit])), axis=0, keepdims=True), 1e-30)
            accum = sum(f * v for f, v in zip(factors, accs))
            reach = jnp.maximum(jnp.max(jnp.abs(accum), axis=0, keepdims=True), 1e-30)
            whole = jnp.round(accum * (STEPS / reach)).astype(jnp.int32)
            lse = top + jnp.log(total)
            scale = reach / (STEPS * total)
            for n in range(2):
                h = 2 * pair + n
                lanes = slice(n * HALF, (n + 1) * HALF)
                sbuf[half, i, h * WIDTH : (h + 1) * WIDTH, :] = whole[:, lanes].astype(jnp.int16)
                sstat[half, i, h : h + 1, :] = lse[:, lanes]
                sstat[half, i, HEADS + h : HEADS + h + 1, :] = scale[:, lanes]

        phase_scores(0)
        phase_scores(1)
        phase_weights(0)
        phase_scores(2)
        phase_weights(1)
        phase_values(0)
        phase_scores(3)
        phase_weights(2)
        phase_values(1)
        phase_weights(3)
        phase_values(2)
        phase_values(3)

        for i in rows_i:
            at_home = diagonal & (i == r)

            @pl.when(at_home)
            def _():
                pltpu.make_async_copy(sbuf.at[half, i], rbuf.at[half, m], home_ls.at[half]).start()
                pltpu.make_async_copy(sstat.at[half, i], rstat.at[half, m], stat_ls.at[half]).start()

            @pl.when(jnp.logical_not(at_home))
            def _():
                remote(sstat.at[half, i], rstat.at[half, m], stat_ss.at[half, i], stat_rs.at[half, m], (i, r * 2 + e)).start()
                remote(sbuf.at[half, i], rbuf.at[half, m], home_ss.at[half, i], home_rs.at[half, m], (i, r * 2 + e)).start()

        return carry

    for half in range(2):
        lax.fori_loop(0, NR // 2, functools.partial(step, half), 0)

    gatesT = contract(wgT[...], own[...], 1, 1).astype(BF16).astype(F32)
    gates = 1.0 / (1.0 + jnp.exp(-gatesT))
    loads[3].wait()

    def home_arrived(half, k):
        is_self = diagonal & (m == k)

        @pl.when(is_self)
        def _():
            pltpu.make_async_copy(sbuf.at[half, k], rbuf.at[half, k], home_ls.at[half]).wait()
            pltpu.make_async_copy(sstat.at[half, k], rstat.at[half, k], stat_ls.at[half]).wait()

        @pl.when(jnp.logical_not(is_self))
        def _():
            remote(sbuf.at[half, k], rbuf.at[half, k], home_ss.at[half, k], home_rs.at[half, k], sib_dev).wait_recv()
            remote(sstat.at[half, k], rstat.at[half, k], stat_ss.at[half, k], stat_rs.at[half, k], sib_dev).wait_recv()

    def merge(half, group, so_far):
        out = []
        for h in range(HEADS):
            low = h * WIDTH
            tops = [rstat[half, k, h : h + 1, :] for k in group]
            if so_far is not None:
                tops.append(so_far[h][0])
            top = functools.reduce(jnp.maximum, tops)
            factors = [jnp.exp(v - top) for v in tops]
            total = sum(factors[: len(group)])
            if so_far is not None:
                total = total + factors[-1] * so_far[h][1]
            accum = sum(
                (f * rstat[half, k, HEADS + h : HEADS + h + 1, :]) * rbuf[half, k, low : low + WIDTH, :].astype(jnp.int32).astype(F32)
                for k, f in zip(group, factors)
            )
            if so_far is not None:
                accum = accum + factors[-1] * merged[low : low + WIDTH, :]
            out.append((top, total, accum))
        return out

    senders = [((r // NYH - a + NZ) % NZ) * NYH + (r + b) % NYH for b in range(NYH) for a in range(NZ)]
    for half in range(2):
        for k in senders[:6]:
            home_arrived(half, k)
        begun = merge(half, senders[:6], None)
        for h in range(HEADS):
            merged[h * WIDTH : (h + 1) * WIDTH, :] = begun[h][2]
        for k in senders[6:]:
            home_arrived(half, k)
        gated = [
            (gates[h * WIDTH : (h + 1) * WIDTH, half * HALF : (half + 1) * HALF] * (accum / total)).astype(BF16)
            for h, (top, total, accum) in enumerate(merge(half, senders[6:], begun))
        ]
        gatedT = jnp.concatenate(gated, axis=0)
        out_ref[0, half * HALF : (half + 1) * HALF, :] = contract(gatedT, w_out_ref[...], 0, 0).astype(BF16)

    for send in kv_sends + kv_ons + first + second + q_ons:
        send.wait_send()
    bias_send.wait_send()

    @pl.when(jnp.logical_not(diagonal))
    def _():
        for send in t_sends:
            send.wait_send()

    for k in range(NR):
        remote(own, nbuf.at[k, e], sib_ss.at[k], sib_rs.at[k], sib_dev).wait_send()

        @pl.when(jnp.logical_not(diagonal & (m == k)))
        def _():
            for half in range(2):
                remote(sbuf.at[half, k], rbuf.at[half, k], home_ss.at[half, k], home_rs.at[half, k], sib_dev).wait_send()
                remote(sstat.at[half, k], rstat.at[half, k], stat_ss.at[half, k], stat_rs.at[half, k], sib_dev).wait_send()


def local(pair_window, ln_gain, w_proj, w_out, pair_bias, chain_starts, chain_pads, residue_mask):
    vmem = pl.BlockSpec(memory_space=pltpu.VMEM)
    smem = pl.BlockSpec(memory_space=pltpu.SMEM)
    hbm = pl.BlockSpec(memory_space=pl.ANY)
    dma = pltpu.SemaphoreType.DMA
    return pl.pallas_call(
        kernel,
        out_shape=pltpu.VMEM((1, CHUNK, CH), BF16),
        in_specs=[smem, smem] + [hbm] * 6,
        out_specs=vmem,
        scratch_shapes=[
            pltpu.VMEM((1, CHUNK, CH), BF16),
            pltpu.VMEM((1, CH), F32),
            pltpu.VMEM((CH, 4 * CH), BF16),
            pltpu.VMEM((CH, CH), BF16),
            pltpu.VMEM((LENGTH // KEYBLK, KEYBLK), jnp.int32),
            pltpu.VMEM((NR, 2, CHUNK, CH), BF16),
            pltpu.VMEM((NR, CHUNK, CH), BF16),
            pltpu.VMEM((NR, KEYS, CH), BF16),
            pltpu.VMEM((NR, CH, KEYS), BF16),
            pltpu.VMEM((2, HEADS, CHUNK, CHUNK), BF16),
            pltpu.VMEM((2, HEADS // 2, KEYS, CHUNK), F32),
            pltpu.VMEM((CHUNK, CH), BF16),
            pltpu.VMEM((CH, CH), BF16),
            pltpu.VMEM((CH, CH), BF16),
            pltpu.VMEM((CH, CH), BF16),
            pltpu.VMEM((HEADS, KEYS, CHUNK), F32),
            pltpu.VMEM((HEADS, KEYS, CHUNK), BF16),
            pltpu.VMEM((2, NR, CH, HALF), jnp.int16),
            pltpu.VMEM((2, NR, STATS, HALF), F32),
            pltpu.VMEM((2, NM, CH, HALF), jnp.int16),
            pltpu.VMEM((2, NM, STATS, HALF), F32),
            pltpu.VMEM((CH, HALF), F32),
            dma((5,)), dma((7,)), dma((NR,)), dma((NR,)), dma((NR,)), dma((2, 7)), dma((2, NR)), dma((2,)), dma, dma, dma,
            dma((2, NR)), dma((2, NM)), dma((2,)), dma((2, NR)), dma((2, NM)), dma((2,)),
        ],
        compiler_params=pltpu.CompilerParams(
            collective_id=0, has_side_effects=True, vmem_limit_bytes=60 * 2**20
        ),
        name="triangle",
    )(
        chain_starts, chain_pads, pair_window, ln_gain.reshape(1, CH), w_proj, w_out,
        residue_mask.reshape(LENGTH // KEYBLK, KEYBLK), pair_bias,
    )


def solution(mesh):
    in_specs = (P("row", "key", None), P(), P(), P(), P(None, "row", "key"), P(), P(), P())
    out_specs = P("row", "key", None)
    return jax.shard_map(local, mesh=mesh, in_specs=in_specs, out_specs=out_specs, check_vma=False)
```

```python
import functools

import jax
import jax.numpy as jnp
from jax import lax
from jax.experimental import pallas as pl
from jax.experimental.pallas import tpu as pltpu
from jax.sharding import PartitionSpec as P

HEADS = 4
KEYBLK = 128
WIDTH = 32
CH = 128
CHUNK = 256
KEYS = 2 * CHUNK
NBLK = KEYS // KEYBLK
NX, NYL, NZ, NYH = 4, 2, 4, 2
NR = NX * NYL
NM = NZ * NYH
NCHAIN = 4
LENGTH = 4096
STATS = 3 * HEADS
HALF = CHUNK // 2
STEPS = 32767.0
MESH = pl.DeviceIdType.MESH
F32 = jnp.float32
BF16 = jnp.bfloat16

epsilon = 1e-05
dead_score = -1000000000.0
dead_bias = -1e30


def contract(a, b, dim_a, dim_b):
    return lax.dot_general(a, b, (((dim_a,), (dim_b,)), ((), ())), preferred_element_type=F32)


OTHERS = ((2, 1), (1, 1), (3, 1), (2, 0), (0, 1), (1, 0), (3, 0))


def kernel(
    starts_ref, pads_ref, x_hbm, gain_hbm, w_hbm, w_out_hbm, mask_hbm, bias_ref, out_ref,
    x_ref, gain_ref, w_ref, w_out_ref, mask_ref,
    nbuf, qbuf, kbuf, vbuf, braw, biasT, own, wqT, wvT, wgT, s_scr, p_scr, sbuf, sstat, rbuf, rstat, merged,
    in_sem, kv_ss, kv_rs, sib_ss, sib_rs, q_ss, q_rs, t_ss, bias_ss, bias_rs, bias_ls, home_ss, home_rs, home_ls,
    stat_ss, stat_rs, stat_ls,
):
    r = lax.axis_index("row")
    c = lax.axis_index("key")
    m = c // 2
    e = c % 2
    x, yl = r % NX, r // NX
    z, yh = m // NYH, m % NYH
    row_at = lambda a, b: ((yl + b) % NYL) * NX + (x + a) % NX
    key_at = lambda a, b: ((z + a) % NZ) * NYH + (yh + b) % NYH
    row_dev = lambda a, b: (row_at(a, b), c)
    key_dev = lambda a, b: (r, key_at(a, b) * 2 + e)
    sib_dev = (r, m * 2 + 1 - e)
    diagonal = r == m

    def remote(src, dst, ss, rs, device):
        return pltpu.make_async_remote_copy(
            src_ref=src, dst_ref=dst, send_sem=ss, recv_sem=rs, device_id=device, device_id_type=MESH
        )

    loads = [
        pltpu.make_async_copy(src, dst, in_sem.at[n])
        for n, (src, dst) in enumerate(
            ((x_hbm, x_ref), (gain_hbm, gain_ref), (w_hbm, w_ref), (w_out_hbm, w_out_ref), (mask_hbm, mask_ref))
        )
    ]
    loads[0].start()
    loads[1].start()
    local_bias = pltpu.make_async_copy(bias_ref.at[:, pl.ds(pl.multiple_of(e * CHUNK, CHUNK), CHUNK), :], braw.at[e], bias_ls)

    barrier = pltpu.get_barrier_semaphore()
    def greet(device):
        pl.semaphore_signal(barrier, inc=1, device_id=device, device_id_type=MESH)

    greet(sib_dev)

    @pl.when(jnp.logical_not(diagonal))
    def _():
        greet((m, r * 2 + e))

    for a, b in OTHERS:
        greet(row_dev(a, b))
        greet(key_dev(a, b))

    for load in loads[2:] + [local_bias]:
        load.start()

    loads[0].wait()
    loads[1].wait()
    values = x_ref[0].astype(F32)
    average = jnp.mean(values, axis=-1, keepdims=True)
    centred = values - average
    variance = jnp.mean(centred * centred, axis=-1, keepdims=True)
    normed = (centred * lax.rsqrt(variance + epsilon) * gain_ref[...]).astype(BF16)
    own[...] = normed
    nbuf[r, e] = normed

    pl.semaphore_wait(barrier, 15 + jnp.where(diagonal, 0, 1))

    halves = [pl.ds(n * HALF, HALF) for n in range(2)]
    t_sends = [remote(own.at[v], qbuf.at[r, v], t_ss.at[n], q_rs.at[n, r], (m, r * 2 + e)) for n, v in enumerate(halves)]

    @pl.when(jnp.logical_not(diagonal))
    def _():
        for send in t_sends:
            send.start()

    @pl.when(diagonal)
    def _():
        qbuf[r] = own[...]

    partner = row_at(0, 1)
    kv_sends = [remote(own, nbuf.at[r, e], kv_ss.at[0], kv_rs.at[r], row_dev(0, 1))]
    kv_sends += [remote(own, nbuf.at[r, e], kv_ss.at[a], kv_rs.at[r], row_dev(a, 0)) for a in (1, 3, 2)]
    for send in kv_sends:
        send.start()
    remote(own, nbuf.at[r, e], sib_ss.at[r], sib_rs.at[r], sib_dev).start()
    bias_send = remote(
        bias_ref.at[:, pl.ds(pl.multiple_of((1 - e) * CHUNK, CHUNK), CHUNK), :], braw.at[e], bias_ss, bias_rs, sib_dev
    )
    bias_send.start()

    def arrived(i):
        remote(own, nbuf.at[i, e], kv_ss.at[0], kv_rs.at[i], sib_dev).wait_recv()

    def to_sibling(i):
        arrived(i)
        remote(nbuf.at[i, e], nbuf.at[i, e], sib_ss.at[i], sib_rs.at[i], sib_dev).start()

    loads[2].wait()
    for ref, low in ((wqT, 0), (wvT, 2 * CH), (wgT, 3 * CH)):
        ref[...] = w_ref[:, low : low + CH].astype(F32).T.astype(BF16)
    loads[4].wait()

    def turn_bias(core):
        for b in range(2):
            key0 = m * KEYS + core * CHUNK + b * KEYBLK
            place = key0 + lax.broadcasted_iota(jnp.int32, (1, KEYBLK), 1)
            inside = jnp.zeros((1, KEYBLK), jnp.bool_)
            leading = jnp.zeros((1, KEYBLK), jnp.bool_)
            for n in range(NCHAIN):
                start = starts_ref[n]
                end = (starts_ref[n + 1] if n < NCHAIN - 1 else LENGTH) - pads_ref[n]
                inside = inside | ((place >= start) & (place < end))
                leading = leading | (place == start)
            alive = inside & ((mask_ref[pl.ds(m * NBLK + core * 2 + b, 1), :] == 1) | leading)
            for h in range(HEADS):
                piece = braw[core, h, :, b * KEYBLK : (b + 1) * KEYBLK].astype(F32)
                piece = jnp.where(alive, piece, dead_bias)
                turned = piece.T
                for n in range(2):
                    biasT[
                        n, h // 2, pl.ds(pl.multiple_of(core * CHUNK + b * KEYBLK, KEYBLK), KEYBLK), (h % 2) * HALF : (h % 2 + 1) * HALF
                    ] = turned[:, n * HALF : (n + 1) * HALF]

    local_bias.wait()
    turn_bias(e)

    arrived(partner)
    kv_ons = [remote(nbuf.at[partner, e], nbuf.at[partner, e], kv_ss.at[3 + a], kv_rs.at[partner], row_dev(a, 0)) for a in (1, 3, 2)]
    for send in kv_ons:
        send.start()
    remote(nbuf.at[partner, e], nbuf.at[partner, e], sib_ss.at[partner], sib_rs.at[partner], sib_dev).start()

    def q_arrived(i, n):
        remote(own.at[halves[n]], qbuf.at[i, halves[n]], t_ss.at[0], q_rs.at[n, i], sib_dev).wait_recv()

    def q_copy(i, n, slot, device):
        v = qbuf.at[i, halves[n]]
        return remote(v, v, q_ss.at[n, slot], q_rs.at[n, i], device)

    def share(n):
        @pl.when(jnp.logical_not(diagonal))
        def _():
            q_arrived(m, n)

        now = [q_copy(m, n, 0, key_dev(0, 1))] + [q_copy(m, n, a, key_dev(a, 0)) for a in (1, 3, 2)]
        for send in now:
            send.start()
        return now

    first = share(0)
    bias_send.wait_recv()
    turn_bias(1 - e)
    second = share(1)
    for a, b in ((1, 0), (3, 0), (2, 0), (1, 1), (3, 1), (2, 1)):
        to_sibling(row_at(a, b))

    other = key_at(0, 1)
    q_ons = []
    for n in range(2):
        q_arrived(other, n)
        now = [q_copy(other, n, 3 + a, key_dev(a, 0)) for a in (1, 3, 2)]
        for send in now:
            send.start()
        q_ons += now

    def turn(s):
        return ((z + s) % NZ) * NYH + (yh + s // NZ) % NYH

    def step(half, count, carry):
        q_half = halves[half]
        places = [2 * count + u for u in range(2)]
        rows_i = [turn(s) for s in places]

        for s, i in zip(places, rows_i):
            if half == 0:
                remote(own, nbuf.at[i, 1 - e], kv_ss.at[0], sib_rs.at[i], sib_dev).wait_recv()

            @pl.when((s > 0) & (s != NZ))
            def _():
                remote(own.at[q_half], qbuf.at[i, q_half], t_ss.at[0], q_rs.at[half, i], sib_dev).wait_recv()

        if half == 0:
            for i in rows_i:
                rows = nbuf[i].reshape(KEYS, CH)
                kbuf[i] = jnp.dot(rows, w_ref[:, CH : 2 * CH], preferred_element_type=F32).astype(BF16)
                vbuf[i] = contract(wvT[...], rows, 1, 1).astype(BF16)

        queriesT = [(contract(wqT[...], qbuf[i, q_half, :], 1, 1) * (WIDTH**-0.5)).astype(BF16) for i in rows_i]
        tops, sums = {}, {}

        def one_head(u, h):
            low = h * WIDTH
            parts = []
            if low:
                parts.append(jnp.zeros((low, HALF), BF16))
            parts.append(queriesT[u][low : low + WIDTH])
            if low + WIDTH < CH:
                parts.append(jnp.zeros((CH - low - WIDTH, HALF), BF16))
            return jnp.concatenate(parts, axis=0)

        def phase_scores(unit):
            u, pair = unit // 2, unit % 2
            both = jnp.concatenate([one_head(u, 2 * pair), one_head(u, 2 * pair + 1)], axis=1)
            scores = jnp.dot(kbuf[rows_i[u]], both, preferred_element_type=F32)
            tops[unit] = []
            for b in range(NBLK):
                k0 = b * KEYBLK
                part = scores[k0 : k0 + KEYBLK] + biasT[half, pair, k0 : k0 + KEYBLK, :]
                s_scr[unit, k0 : k0 + KEYBLK, :] = part
                tops[unit].append(jnp.maximum(jnp.max(part, axis=0, keepdims=True), dead_score))

        def phase_weights(unit):
            sums[unit] = []
            for b in range(NBLK):
                k0 = b * KEYBLK
                weights = jnp.exp(s_scr[unit, k0 : k0 + KEYBLK, :] - tops[unit][b])
                sums[unit].append(jnp.sum(weights.reshape(KEYBLK // 8, 8, CHUNK), axis=0))
                p_scr[unit, k0 : k0 + KEYBLK, :] = weights.astype(BF16)

        def phase_values(unit):
            u, pair = unit // 2, unit % 2
            i = rows_i[u]
            low = 2 * pair * WIDTH
            accs = []
            for b in range(NBLK):
                k0 = b * KEYBLK
                both = jnp.dot(
                    vbuf[i, low : low + 2 * WIDTH, k0 : k0 + KEYBLK], p_scr[unit, k0 : k0 + KEYBLK, :], preferred_element_type=F32
                )
                accs.append(jnp.concatenate([both[:WIDTH, :HALF], both[WIDTH:, HALF:]], axis=1))
            top = functools.reduce(jnp.maximum, tops[unit])
            factors = [jnp.exp(v - top) for v in tops[unit]]
            total = jnp.sum(sum(f * v for f, v in zip(factors, sums[unit])), axis=0, keepdims=True)
            accum = sum(f * v for f, v in zip(factors, accs))
            reach = jnp.maximum(jnp.max(jnp.abs(accum), axis=0, keepdims=True), 1e-30)
            whole = jnp.round(accum * (STEPS / reach)).astype(jnp.int32)
            scale = reach * (1.0 / STEPS)
            for n in range(2):
                h = 2 * pair + n
                lanes = slice(n * HALF, (n + 1) * HALF)
                sbuf[half, i, h * WIDTH : (h + 1) * WIDTH, :] = whole[:, lanes].astype(jnp.int16)
                for row, value in enumerate((top, total, scale)):
                    sstat[half, i, row * HEADS + h : row * HEADS + h + 1, :] = value[:, lanes]

        phase_scores(0)
        phase_scores(1)
        phase_weights(0)
        phase_scores(2)
        phase_weights(1)
        phase_values(0)
        phase_scores(3)
        phase_weights(2)
        phase_values(1)
        phase_weights(3)
        phase_values(2)
        phase_values(3)

        for i in rows_i:
            at_home = diagonal & (i == r)

            @pl.when(at_home)
            def _():
                pltpu.make_async_copy(sbuf.at[half, i], rbuf.at[half, m], home_ls.at[half]).start()
                pltpu.make_async_copy(sstat.at[half, i], rstat.at[half, m], stat_ls.at[half]).start()

            @pl.when(jnp.logical_not(at_home))
            def _():
                remote(sstat.at[half, i], rstat.at[half, m], stat_ss.at[half, i], stat_rs.at[half, m], (i, r * 2 + e)).start()
                remote(sbuf.at[half, i], rbuf.at[half, m], home_ss.at[half, i], home_rs.at[half, m], (i, r * 2 + e)).start()

        return carry

    for half in range(2):
        lax.fori_loop(0, NR // 2, functools.partial(step, half), 0)

    gatesT = contract(wgT[...], own[...], 1, 1).astype(BF16).astype(F32)
    gates = 1.0 / (1.0 + jnp.exp(-gatesT))
    loads[3].wait()

    def home_arrived(half, k):
        is_self = diagonal & (m == k)

        @pl.when(is_self)
        def _():
            pltpu.make_async_copy(sbuf.at[half, k], rbuf.at[half, k], home_ls.at[half]).wait()
            pltpu.make_async_copy(sstat.at[half, k], rstat.at[half, k], stat_ls.at[half]).wait()

        @pl.when(jnp.logical_not(is_self))
        def _():
            remote(sbuf.at[half, k], rbuf.at[half, k], home_ss.at[half, k], home_rs.at[half, k], sib_dev).wait_recv()
            remote(sstat.at[half, k], rstat.at[half, k], stat_ss.at[half, k], stat_rs.at[half, k], sib_dev).wait_recv()

    def merge(half, group, so_far):
        out = []
        for h in range(HEADS):
            low = h * WIDTH
            tops = [rstat[half, k, h : h + 1, :] for k in group]
            if so_far is not None:
                tops.append(so_far[h][0])
            top = functools.reduce(jnp.maximum, tops)
            factors = [jnp.exp(v - top) for v in tops]
            total = sum(f * rstat[half, k, HEADS + h : HEADS + h + 1, :] for k, f in zip(group, factors))
            if so_far is not None:
                total = total + factors[-1] * so_far[h][1]
            accum = sum(
                (f * rstat[half, k, 2 * HEADS + h : 2 * HEADS + h + 1, :]) * rbuf[half, k, low : low + WIDTH, :].astype(jnp.int32).astype(F32)
                for k, f in zip(group, factors)
            )
            if so_far is not None:
                accum = accum + factors[-1] * merged[low : low + WIDTH, :]
            out.append((top, total, accum))
        return out

    senders = [((r // NYH - a + NZ) % NZ) * NYH + (r + b) % NYH for b in range(NYH) for a in range(NZ)]
    for half in range(2):
        for k in senders[:6]:
            home_arrived(half, k)
        begun = merge(half, senders[:6], None)
        for h in range(HEADS):
            merged[h * WIDTH : (h + 1) * WIDTH, :] = begun[h][2]
        for k in senders[6:]:
            home_arrived(half, k)
        gated = [
            (gates[h * WIDTH : (h + 1) * WIDTH, half * HALF : (half + 1) * HALF] * (accum / total)).astype(BF16)
            for h, (top, total, accum) in enumerate(merge(half, senders[6:], begun))
        ]
        gatedT = jnp.concatenate(gated, axis=0)
        out_ref[0, half * HALF : (half + 1) * HALF, :] = contract(gatedT, w_out_ref[...], 0, 0).astype(BF16)

    for send in kv_sends + kv_ons + first + second + q_ons:
        send.wait_send()
    bias_send.wait_send()

    @pl.when(jnp.logical_not(diagonal))
    def _():
        for send in t_sends:
            send.wait_send()

    for k in range(NR):
        remote(own, nbuf.at[k, e], sib_ss.at[k], sib_rs.at[k], sib_dev).wait_send()

        @pl.when(jnp.logical_not(diagonal & (m == k)))
        def _():
            for half in range(2):
                remote(sbuf.at[half, k], rbuf.at[half, k], home_ss.at[half, k], home_rs.at[half, k], sib_dev).wait_send()
                remote(sstat.at[half, k], rstat.at[half, k], stat_ss.at[half, k], stat_rs.at[half, k], sib_dev).wait_send()


def local(pair_window, ln_gain, w_proj, w_out, pair_bias, chain_starts, chain_pads, residue_mask):
    vmem = pl.BlockSpec(memory_space=pltpu.VMEM)
    smem = pl.BlockSpec(memory_space=pltpu.SMEM)
    hbm = pl.BlockSpec(memory_space=pl.ANY)
    dma = pltpu.SemaphoreType.DMA
    return pl.pallas_call(
        kernel,
        out_shape=pltpu.VMEM((1, CHUNK, CH), BF16),
        in_specs=[smem, smem] + [hbm] * 6,
        out_specs=vmem,
        scratch_shapes=[
            pltpu.VMEM((1, CHUNK, CH), BF16),
            pltpu.VMEM((1, CH), F32),
            pltpu.VMEM((CH, 4 * CH), BF16),
            pltpu.VMEM((CH, CH), BF16),
            pltpu.VMEM((LENGTH // KEYBLK, KEYBLK), jnp.int32),
            pltpu.VMEM((NR, 2, CHUNK, CH), BF16),
            pltpu.VMEM((NR, CHUNK, CH), BF16),
            pltpu.VMEM((NR, KEYS, CH), BF16),
            pltpu.VMEM((NR, CH, KEYS), BF16),
            pltpu.VMEM((2, HEADS, CHUNK, CHUNK), BF16),
            pltpu.VMEM((2, HEADS // 2, KEYS, CHUNK), F32),
            pltpu.VMEM((CHUNK, CH), BF16),
            pltpu.VMEM((CH, CH), BF16),
            pltpu.VMEM((CH, CH), BF16),
            pltpu.VMEM((CH, CH), BF16),
            pltpu.VMEM((HEADS, KEYS, CHUNK), F32),
            pltpu.VMEM((HEADS, KEYS, CHUNK), BF16),
            pltpu.VMEM((2, NR, CH, HALF), jnp.int16),
            pltpu.VMEM((2, NR, STATS, HALF), F32),
            pltpu.VMEM((2, NM, CH, HALF), jnp.int16),
            pltpu.VMEM((2, NM, STATS, HALF), F32),
            pltpu.VMEM((CH, HALF), F32),
            dma((5,)), dma((7,)), dma((NR,)), dma((NR,)), dma((NR,)), dma((2, 7)), dma((2, NR)), dma((2,)), dma, dma, dma,
            dma((2, NR)), dma((2, NM)), dma((2,)), dma((2, NR)), dma((2, NM)), dma((2,)),
        ],
        compiler_params=pltpu.CompilerParams(
            collective_id=0, has_side_effects=True, vmem_limit_bytes=60 * 2**20
        ),
        name="triangle",
    )(
        chain_starts, chain_pads, pair_window, ln_gain.reshape(1, CH), w_proj, w_out,
        residue_mask.reshape(LENGTH // KEYBLK, KEYBLK), pair_bias,
    )


def solution(mesh):
    in_specs = (P("row", "key", None), P(), P(), P(), P(None, "row", "key"), P(), P(), P())
    out_specs = P("row", "key", None)
    return jax.shard_map(local, mesh=mesh, in_specs=in_specs, out_specs=out_specs, check_vma=False)
```
